256 devices in a mesh: block: 8 (over x, core), space: 32 (over y, z).
Axes of the slice: x: 4, y: 4, z: 8, core: 2. Of those that a mesh axis runs over, the one named last changes fastest.
Arguments:
- snapshots: bfloat16 [32, 32, 2, 256, 3, 256], P('space', None, None, 'block'), may hold values from -6 to 6
- slot_line: int32 [32, 32, 2], replicated, may hold values from -1 to 31, as said below
- freq_ids: int32 [24], replicated, may hold values from 0 to 128, as said below
- metrics: float32 [4, 128, 256], P(None, 'space'), may hold values from -1.5 to 1.5
- weights: float32 [128, 256], P('space'), may hold values from 0.25 to 12, as said below
- stored_spectra: bfloat16 [24, 2, 2, 3, 128, 8, 256], P('block', None, None, None, 'space'), may hold values from -6 to 6
Outputs:
- spectra: bfloat16 [24, 2, 3, 128, 8, 256], P('block', None, None, 'space')
- gram: float32 [24, 2, 3, 3], P('block')
The draws below stay inside these ranges and needn't reach their ends.
Inputs may be any that keep to these rules, and one draw needn't show every extreme that they name: slot_line[h, d, s] is the local index (pitch-major, 8 per pitch line) of the owner d line that holder h keeps in slot s, or -1 for an empty slot. Each of an owner's 32 lines stands in exactly one slot; for every owner some holder fills all 2 of its slots. `freq_ids`: distinct values. `weights`: Positive.
All inputs are finite; a program needn't handle non-finite values.
Results may differ from the reference program's by a relative error of at most 0.008.
Values may be sent and summed in bfloat16 or wider, within the bound.
No kernel may reach another device: no remote copies, remote signals or barrier semaphores. Data moves between devices by JAX's collectives and lax.ppermute only.
A program may use at most 320 MiB of HBM per device.

```python
import math
import jax
import jax.numpy as jnp
from jax import lax

P_SIZE = 256
NT = 256
NF = 24
NK = 8
NOLD = 2
NCOL = 3
NJ = 128
LD = 32
C = 2
N_SPACE = 32


def draw_slot_line(key, part):
    slot_count = N_SPACE * C
    first, second, third = jax.random.split(key, 3)
    urgency = jax.random.randint(first, (N_SPACE,), 0, 4)
    jitter = jax.random.randint(second, (N_SPACE, N_SPACE, C), 0, 4 * slot_count)
    chosen = jax.random.randint(third, (N_SPACE,), 0, N_SPACE)
    holder = jnp.arange(N_SPACE, dtype=jnp.int32)
    score = urgency[None, :, None] * (4 * slot_count) + jitter
    score = score + jnp.where(holder[None, :, None] == chosen[:, None, None], 16 * slot_count, 0)
    flat = score.reshape(N_SPACE, slot_count) * slot_count + jnp.arange(slot_count, dtype=jnp.int32)[None, :]
    order = jnp.argsort(-flat, axis=1)
    ranking = jnp.argsort(order, axis=1).astype(jnp.int32)
    line_ids = jnp.where(ranking < LD, ranking, -1).astype(jnp.int32)
    return jnp.transpose(line_ids.reshape(N_SPACE, N_SPACE, C), (1, 0, 2))


def draw_freq_ids(key, part):
    return jax.random.permutation(key, NT // 2 + 1)[:NF].astype(jnp.int32)


def draw_weights(key, part):
    pitch = jnp.arange(NJ, dtype=jnp.float32)[:, None]
    rising = jnp.exp(math.log(3.0) * pitch / max(NJ - 1, 1))
    rough = jax.random.uniform(key, (NJ, P_SIZE), minval=0.5, maxval=2.0)
    return (rising * rough).astype(jnp.float32)


def draw_stored_spectra(key, part):
    key = jax.random.fold_in(key, 7)
    common_key, noise_key, phase_key, mix_key = jax.random.split(key, 4)
    common_shape = (NF, 1, 2, 3, NJ, NK, P_SIZE)
    noise_shape = (NF, NOLD, 2, 3, NJ, NK, P_SIZE)
    common = jax.random.normal(common_key, common_shape)
    noise = jax.random.normal(noise_key, noise_shape)
    phase = jax.random.uniform(phase_key, (NF, NOLD), minval=-math.pi, maxval=math.pi)
    mix = jax.random.uniform(mix_key, (NF, 1), minval=0.5, maxval=0.9)
    cosine = (mix * jnp.cos(phase))[:, :, None, None, None, None]
    sine = (mix * jnp.sin(phase))[:, :, None, None, None, None]
    real_common = common[:, :, 0]
    imag_common = common[:, :, 1]
    turned_real = cosine * real_common - sine * imag_common
    turned_imag = sine * real_common + cosine * imag_common
    turned = jnp.stack([turned_real, turned_imag], axis=2)
    rest = jnp.sqrt(1.0 - mix * mix)[:, :, None, None, None, None, None]
    values = jnp.clip(turned + rest * noise, -6.0, 6.0)
    return values.astype(jnp.bfloat16)


def level_of(stream_key, extent, cuts, smallest, high):
    loudness = 1.0
    for dim, parts in cuts:
        steps = jax.random.uniform(jax.random.fold_in(jax.random.fold_in(stream_key, 6), dim), (parts,), jnp.float32, smallest / len(cuts), high / len(cuts))
        loudness = loudness * jnp.repeat(jnp.exp(steps), extent[dim] // parts).reshape((-1,) + (1,) * (len(extent) - 1 - dim))
    return loudness


def normal_values(rng, extent, deviation, reach, pieces=(), kind=jnp.bfloat16):
    values = deviation * jax.random.normal(rng, extent, jnp.float32)
    if pieces:
        values = values * level_of(rng, extent, pieces, -0.22, 0.18)
    return jnp.clip(values, -reach, reach).astype(kind)


def setup_inputs(seed: int = 0) -> dict:
    keys = jax.random.split(jax.random.key(seed), 7)
    snapshots = normal_values(keys[0], (N_SPACE, N_SPACE, C, NT, 3, P_SIZE), 1.0, 6.0, ((0, 32), (3, 8)))
    slot_line = draw_slot_line(jax.random.fold_in(keys[6], 71), 0)
    freq_ids = draw_freq_ids(jax.random.fold_in(keys[6], 71), 0)
    metrics = jnp.clip(jax.random.uniform(keys[3], (4, NJ, P_SIZE), jnp.float32, -1.5, 1.5) * level_of(keys[3], (4, NJ, P_SIZE), ((1, 32),), -0.4, 0.0), -1.5, 1.5)
    weights = draw_weights(jax.random.fold_in(keys[6], 71), 0)
    stored_spectra = draw_stored_spectra(jax.random.fold_in(keys[6], 71), 0)
    return dict(snapshots=snapshots, slot_line=slot_line, freq_ids=freq_ids, metrics=metrics, weights=weights, stored_spectra=stored_spectra)


span_metric = 1.0

def fourier_table(freq_ids, times, total):
    turns = times[:, None] * freq_ids[None, :] % total
    theta = 2.0 * math.pi / total * turns.astype(jnp.float32)
    window = 0.5 - 0.5 * jnp.cos(2.0 * math.pi / total * times.astype(jnp.float32))
    scale = 1.0 / math.sqrt(0.375 * total)
    cosine = scale * window[:, None] * jnp.cos(theta)
    sine = -scale * window[:, None] * jnp.sin(theta)
    table = jnp.stack([cosine, sine], axis=-1)
    return table.reshape(times.shape[0], -1).astype(jnp.bfloat16)

def line_derivative(field):
    inner = (field[..., :-4] - 8.0 * field[..., 1:-3] + 8.0 * field[..., 3:-1] - field[..., 4:]) / 12.0
    first = (-25.0 * field[..., 0] + 48.0 * field[..., 1] - 36.0 * field[..., 2] + 16.0 * field[..., 3] - 3.0 * field[..., 4]) / 12.0
    second = (-3.0 * field[..., 0] - 10.0 * field[..., 1] + 18.0 * field[..., 2] - 6.0 * field[..., 3] + field[..., 4]) / 12.0
    penult = (3.0 * field[..., -1] + 10.0 * field[..., -2] - 18.0 * field[..., -3] + 6.0 * field[..., -4] - field[..., -5]) / 12.0
    final = (25.0 * field[..., -1] - 48.0 * field[..., -2] + 36.0 * field[..., -3] - 16.0 * field[..., -4] + 3.0 * field[..., -5]) / 12.0
    return jnp.concatenate([first[..., None], second[..., None], inner, penult[..., None], final[..., None]], axis=-1)

def vorticity(padded, metric):
    center = padded[2:-2]
    along_line = line_derivative(center)
    along_pitch = (padded[:-4] - 8.0 * padded[1:-3] + 8.0 * padded[3:-1] - padded[4:]) / 12.0
    along_span = (jnp.roll(center, 2, axis=1) - 8.0 * jnp.roll(center, 1, axis=1) + 8.0 * jnp.roll(center, -1, axis=1) - jnp.roll(center, -2, axis=1)) * (span_metric / 12.0)
    shape = (metric.shape[1], 1, 1, 1, metric.shape[2])
    xi_x = metric[0].reshape(shape)
    xi_y = metric[1].reshape(shape)
    eta_x = metric[2].reshape(shape)
    eta_y = metric[3].reshape(shape)
    d_x = xi_x * along_line + eta_x * along_pitch
    d_y = xi_y * along_line + eta_y * along_pitch
    omega_x = d_y[:, :, :, 2] - along_span[:, :, :, 1]
    omega_y = along_span[:, :, :, 0] - d_x[:, :, :, 2]
    omega_z = d_x[:, :, :, 1] - d_y[:, :, :, 0]
    return jnp.stack([omega_x, omega_y, omega_z], axis=0)

def reference(snapshots, slot_line, freq_ids, metrics, weights, stored_spectra):
    slot_count = N_SPACE * C
    line_index = jnp.arange(LD, dtype=jnp.int32)
    slot_index = jnp.arange(slot_count, dtype=jnp.int32)

    def assemble(owner):
        held = lax.dynamic_index_in_dim(snapshots, owner, 1, keepdims=False).reshape(slot_count, NT, 3, P_SIZE)
        slot_ids = lax.dynamic_index_in_dim(slot_line, owner, 1, keepdims=False).reshape(slot_count)
        position = lax.optimization_barrier(jnp.sum(jnp.where(slot_ids[None, :] == line_index[:, None], slot_index[None, :], 0), axis=1)).astype(jnp.int32)
        return jnp.take(held, position, axis=0)
    field = lax.map(assemble, jnp.arange(N_SPACE, dtype=jnp.int32)).reshape(NJ, NK, NT, 3, P_SIZE)
    table = fourier_table(freq_ids, jnp.arange(NT, dtype=jnp.int32), NT).astype(jnp.float32)

    def velocity_row(pitch_row):
        line = lax.dynamic_index_in_dim(field, pitch_row, 0, keepdims=False).astype(jnp.float32)
        result = jnp.einsum('tq,ktcp->kqcp', table, line, precision=lax.Precision.HIGHEST)
        return result.astype(jnp.bfloat16)
    velocity_spectra = lax.map(velocity_row, jnp.arange(NJ, dtype=jnp.int32))

    def spectra_row(pitch_row):
        near = (pitch_row + jnp.arange(-2, 3, dtype=jnp.int32)) % NJ
        rows = jnp.take(velocity_spectra, near.astype(jnp.int32), axis=0).astype(jnp.float32)
        metric_row = lax.dynamic_slice_in_dim(metrics, pitch_row, 1, 1)
        vort = vorticity(rows, metric_row).astype(jnp.bfloat16)
        return vort[:, 0]
    rows_out = lax.map(spectra_row, jnp.arange(NJ, dtype=jnp.int32))
    spectra = jnp.transpose(rows_out, (3, 1, 0, 2, 4)).reshape(NF, 2, 3, NJ, NK, P_SIZE)
    npoints = 3.0 * NJ * NK * P_SIZE

    def gram_one(pair):
        fresh, older = pair
        columns = jnp.concatenate([fresh[None], older], axis=0).astype(jnp.float32)
        weighted = columns * weights[:, None, :]
        flat_cols = columns.reshape(2 * NCOL, -1)
        flat_weighted = weighted.reshape(2 * NCOL, -1)
        full = jnp.einsum('am,bm->ab', flat_cols, flat_weighted, precision=lax.Precision.HIGHEST).reshape(NCOL, 2, NCOL, 2)
        real_part = full[:, 0, :, 0] + full[:, 1, :, 1]
        imag_part = full[:, 0, :, 1] - full[:, 1, :, 0]
        return jnp.stack([real_part, imag_part], axis=0) / npoints
    gram = lax.map(gram_one, (spectra, stored_spectra))
    return (spectra, gram)
```

```python
import functools
import math

import jax
import jax.numpy as jnp
import numpy as np
from jax import lax
from jax.experimental import pallas as pl
from jax.experimental.pallas import tpu as pltpu
from jax.sharding import PartitionSpec as P

P_SIZE = 256
NT = 256
NF = 24
NK = 8
JD = 4
LD = JD * NK
ROWS = 40
VMEM = pl.BlockSpec(memory_space=pltpu.VMEM)
PARAMS = pltpu.CompilerParams(vmem_limit_bytes=32 * 1024 * 1024)


def fourier_table(freq_ids, times, total):
    turns = times[:, None] * freq_ids[None, :] % total
    theta = 2.0 * math.pi / total * turns.astype(jnp.float32)
    window = 0.5 - 0.5 * jnp.cos(2.0 * math.pi / total * times.astype(jnp.float32))
    scale = 1.0 / math.sqrt(0.375 * total)
    cosine = scale * window[:, None] * jnp.cos(theta)
    sine = -scale * window[:, None] * jnp.sin(theta)
    table = jnp.stack([cosine, sine], axis=-1)
    return table.reshape(times.shape[0], -1).astype(jnp.bfloat16)


def line_matrix():
    d = np.zeros((P_SIZE, P_SIZE), np.float32)
    for p in range(2, P_SIZE - 2):
        d[p - 2, p], d[p - 1, p], d[p + 1, p], d[p + 2, p] = 1, -8, 8, -1
    first, second = (-25, 48, -36, 16, -3), (-3, -10, 18, -6, 1)
    for i in range(5):
        d[i, 0], d[i, 1] = first[i], second[i]
        d[P_SIZE - 1 - i, P_SIZE - 1], d[P_SIZE - 1 - i, P_SIZE - 2] = -first[i], -second[i]
    return jnp.asarray(d, jnp.bfloat16)


def dft_kernel(raw_ref, table_ref, out_ref):
    blocks, owners = raw_ref.shape[:2]
    for d in range(owners):
        total = None
        for s in range(2):
            for c in range(3):
                lines = raw_ref[:, d, s, c].reshape(NT, P_SIZE)
                term = jnp.dot(
                    table_ref[3 * s + c], lines, preferred_element_type=jnp.float32
                )
                total = term if total is None else total + term
        out_ref[:, d] = total.astype(jnp.bfloat16).reshape(blocks, ROWS, P_SIZE)


def place_kernel(place_ref, held_ref, own_ref, low_ref, high_ref):
    held = held_ref[...].reshape(-1, P_SIZE)
    rows = jnp.dot(place_ref[...], held, preferred_element_type=jnp.float32)
    rows = rows.astype(jnp.bfloat16).reshape(own_ref.shape)
    own_ref[...] = rows
    low_ref[...] = rows[:, :, JD - 2 :]
    high_ref[...] = rows[:, :, :2]


def vorticity_kernel(
    own_ref, low_ref, high_ref, line_ref, metric_ref, weight_ref, stored_ref, spectra_ref, gram_ref
):
    gram_ref[...] = jnp.zeros_like(gram_ref)
    nf = stored_ref.shape[0]
    xi_x, xi_y, eta_x, eta_y = (metric_ref[i].reshape(JD, 1, P_SIZE) for i in range(4))
    weight = weight_ref[...].reshape(1, JD, 1, P_SIZE)
    twelfth = 1.0 / 12.0

    for f in range(nf):
        new = []
        for r in range(2):
            q = 2 * f + r
            d_x, d_y, d_z = [], [], []
            for c in range(3):
                line = own_ref[q, c].reshape(LD, P_SIZE)
                along = jnp.dot(line, line_ref[...], preferred_element_type=jnp.float32)
                along = (along * twelfth).reshape(JD, NK, P_SIZE)
                center = own_ref[q, c].astype(jnp.float32)
                padded = jnp.concatenate(
                    [
                        low_ref[q, c].astype(jnp.float32),
                        center,
                        high_ref[q, c].astype(jnp.float32),
                    ],
                    axis=0,
                )
                pitch = (
                    padded[:-4] - 8.0 * padded[1:-3] + 8.0 * padded[3:-1] - padded[4:]
                ) * twelfth
                span = (
                    pltpu.roll(center, 2, 1)
                    - 8.0 * pltpu.roll(center, 1, 1)
                    + 8.0 * pltpu.roll(center, NK - 1, 1)
                    - pltpu.roll(center, NK - 2, 1)
                ) * twelfth
                d_x.append(xi_x * along + eta_x * pitch)
                d_y.append(xi_y * along + eta_y * pitch)
                d_z.append(span)
            vort = [d_y[2] - d_z[1], d_z[0] - d_x[2], d_x[1] - d_y[0]]
            vort = [v.astype(jnp.bfloat16) for v in vort]
            for c in range(3):
                spectra_ref[f, r, c] = vort[c]
            new.append(jnp.stack([v.astype(jnp.float32) for v in vort], axis=0))
        columns = [tuple(new)] + [
            tuple(stored_ref[f, a, r].astype(jnp.float32) for r in range(2)) for a in range(2)
        ]

        def put(part, a, b, value):
            total = jnp.sum(value, axis=(0, 1, 2)).reshape(1, P_SIZE)
            total = total[:, :128] + total[:, 128:]
            row = ((f * 2 + part) * 3 + a) * 3 + b
            gram_ref[row : row + 1, :] = total
            if a != b:
                row = ((f * 2 + part) * 3 + b) * 3 + a
                gram_ref[row : row + 1, :] = total if part == 0 else -total

        for a in range(3):
            real, imag = (weight * v for v in columns[a])
            for b in range(a, 3):
                put(0, a, b, real * columns[b][0] + imag * columns[b][1])
                if a != b:
                    put(1, a, b, real * columns[b][1] - imag * columns[b][0])


def ring_sum(value, axis, shifts):
    count = lax.axis_size(axis)
    arrived = [lax.ppermute(value, axis, pairs(count)) for pairs in shifts]
    return functools.reduce(lambda a, b: a + b, arrived, value)


def shift_y(k):
    return lambda n: [(i, (i + 8 * k) % n) for i in range(n)]


def shift_z(k):
    return lambda n: [(i, i // 8 * 8 + (i + k) % 8) for i in range(n)]


def per_device(snapshots, slot_line, freq_ids, metrics, weights, stored_spectra):
    groups = lax.axis_size("block")
    holders = lax.axis_size("space")
    owners = holders // groups
    raw = jnp.transpose(snapshots[0], (0, 1, 3, 2, 4))
    raw = raw.reshape((groups, owners) + raw.shape[1:])
    raw = lax.all_to_all(raw, "block", split_axis=0, concat_axis=0, tiled=True)

    table = fourier_table(freq_ids, jnp.arange(NT, dtype=jnp.int32), NT).T
    table = table.reshape(groups, 1, NF // groups * 2, NT)
    table = jnp.broadcast_to(table, (groups, 6, NF // groups * 2, NT)).reshape(groups, 36, NT)
    table = jnp.pad(table, ((0, 0), (0, ROWS - 36), (0, 0)))
    part = jnp.arange(6, dtype=jnp.int32)[:, None, None, None]
    row = jnp.arange(ROWS, dtype=jnp.int32)[None, None, :, None]
    table = jnp.where(row // 6 == part, table[None], 0).reshape(6, groups * ROWS, NT)

    velocity = pl.pallas_call(
        dft_kernel,
        out_shape=jax.ShapeDtypeStruct((groups, owners, ROWS, P_SIZE), jnp.bfloat16),
        in_specs=[VMEM, VMEM],
        out_specs=VMEM,
        compiler_params=PARAMS,
        name="dft",
    )(raw, table)
    velocity = lax.all_to_all(velocity, "block", split_axis=0, concat_axis=0, tiled=True)
    velocity = velocity.reshape(holders, ROWS, P_SIZE)
    velocity = lax.all_to_all(velocity, "space", split_axis=0, concat_axis=0, tiled=True)

    me = lax.axis_index("space")
    ids = lax.dynamic_index_in_dim(slot_line, me, 1, keepdims=False)
    in_row = jnp.arange(ROWS, dtype=jnp.int32)
    held = jnp.where(in_row[None, :] < 18, ids[:, 0:1], ids[:, 1:2])
    inner = in_row % 18
    source = (inner % 6 * 3 + inner // 6)[None, :] * LD + held
    source = jnp.where((held >= 0) & (in_row[None, :] < 36), source, -1).reshape(1, -1)
    target = jnp.arange(18 * LD, dtype=jnp.int32)[:, None]
    place = (source == target).astype(jnp.bfloat16)

    nq = NF // groups * 2
    own, low, high = pl.pallas_call(
        place_kernel,
        out_shape=[
            jax.ShapeDtypeStruct((nq, 3, JD, NK, P_SIZE), jnp.bfloat16),
            jax.ShapeDtypeStruct((nq, 3, 2, NK, P_SIZE), jnp.bfloat16),
            jax.ShapeDtypeStruct((nq, 3, 2, NK, P_SIZE), jnp.bfloat16),
        ],
        in_specs=[VMEM, VMEM],
        out_specs=[VMEM, VMEM, VMEM],
        compiler_params=PARAMS,
        name="place",
    )(place, velocity)
    forward = [(i, (i + 1) % holders) for i in range(holders)]
    backward = [(target, source) for source, target in forward]
    low = lax.ppermute(low, "space", forward)
    high = lax.ppermute(high, "space", backward)

    spectra, gram = pl.pallas_call(
        vorticity_kernel,
        out_shape=[
            jax.ShapeDtypeStruct((NF // groups, 2, 3, JD, NK, P_SIZE), jnp.bfloat16),
            jax.ShapeDtypeStruct((56, 128), jnp.float32),
        ],
        in_specs=[VMEM] * 7,
        out_specs=[VMEM, VMEM],
        compiler_params=PARAMS,
        name="vorticity",
    )(own, low, high, line_matrix(), metrics, weights, stored_spectra)
    gram = jnp.sum(gram, axis=1) * (1.0 / (3.0 * JD * holders * NK * P_SIZE))
    gram = ring_sum(gram, "space", [shift_y(k) for k in range(1, 4)])
    gram = ring_sum(gram, "space", [shift_z(k) for k in range(1, 8)])
    gram = gram[: NF // groups * 18].reshape(NF // groups, 2, 3, 3)
    return (spectra, gram)


def solution(mesh):
    return jax.shard_map(
        per_device,
        mesh=mesh,
        in_specs=(
            P("space", None, None, "block", None, None),
            P(),
            P(),
            P(None, "space", None),
            P("space", None),
            P("block", None, None, None, "space", None, None),
        ),
        out_specs=(P("block", None, None, "space", None, None), P("block", None, None, None)),
        check_vma=False,
    )
```

```python
import functools
import math

import jax
import jax.numpy as jnp
import numpy as np
from jax import lax
from jax.experimental import pallas as pl
from jax.experimental.pallas import tpu as pltpu
from jax.sharding import PartitionSpec as P

P_SIZE = 256
NT = 256
NF = 24
NK = 8
JD = 4
LD = JD * NK
ROWS = 40
PAIR = 72
PARTS = 2
VMEM = pl.BlockSpec(memory_space=pltpu.VMEM)
PARAMS = pltpu.CompilerParams(vmem_limit_bytes=32 * 1024 * 1024)


def fourier_table(freq_ids, times, total):
    turns = times[:, None] * freq_ids[None, :] % total
    theta = 2.0 * math.pi / total * turns.astype(jnp.float32)
    window = 0.5 - 0.5 * jnp.cos(2.0 * math.pi / total * times.astype(jnp.float32))
    scale = 1.0 / math.sqrt(0.375 * total)
    cosine = scale * window[:, None] * jnp.cos(theta)
    sine = -scale * window[:, None] * jnp.sin(theta)
    table = jnp.stack([cosine, sine], axis=-1)
    return table.reshape(times.shape[0], -1).astype(jnp.bfloat16)


def line_matrix():
    d = np.zeros((P_SIZE, P_SIZE), np.float32)
    for p in range(2, P_SIZE - 2):
        d[p - 2, p], d[p - 1, p], d[p + 1, p], d[p + 2, p] = 1, -8, 8, -1
    first, second = (-25, 48, -36, 16, -3), (-3, -10, 18, -6, 1)
    for i in range(5):
        d[i, 0], d[i, 1] = first[i], second[i]
        d[P_SIZE - 1 - i, P_SIZE - 1], d[P_SIZE - 1 - i, P_SIZE - 2] = -first[i], -second[i]
    return jnp.asarray(d, jnp.bfloat16)


def dft_kernel(mine_ref, other_ref, table_ref, own_ref, next_ref, across_ref, last_ref):
    def share(d):
        lines = jnp.concatenate(
            [mine_ref[d].reshape(-1, P_SIZE), other_ref[d].reshape(-1, P_SIZE)], axis=0
        )
        return jnp.dot(table_ref[d % 2], lines, preferred_element_type=jnp.float32)

    for pair in range(own_ref.shape[0]):
        even, odd = share(2 * pair), share(2 * pair + 1)
        for k, ref in enumerate((own_ref, next_ref, across_ref, last_ref)):
            first, second = even[k * ROWS : (k + 1) * ROWS], odd[k * ROWS : (k + 1) * ROWS]
            both = jnp.concatenate(
                [first[: ROWS - 8], first[ROWS - 8 :] + second[:8], second[8:]], axis=0
            )
            ref[pair] = both.astype(ref.dtype)


def sum_kernel(parts, *refs):
    out_ref = refs[-1]
    pair = 0
    for part in range(parts):
        own, a, b, c = refs[4 * part : 4 * part + 4]
        for i in range(own.shape[0]):
            total = own[i] + a[i].astype(jnp.float32)
            total = total + b[i].astype(jnp.float32) + c[i].astype(jnp.float32)
            total = total.astype(jnp.bfloat16)
            out_ref[2 * pair] = total[:ROWS]
            out_ref[2 * pair + 1] = total[PAIR - ROWS :]
            pair += 1


def place_kernel(place_ref, held_ref, own_ref, low_ref, high_ref):
    held = held_ref[...].reshape(-1, P_SIZE)
    rows = jnp.dot(place_ref[...], held, preferred_element_type=jnp.float32)
    rows = rows.astype(jnp.bfloat16).reshape(own_ref.shape)
    own_ref[...] = rows
    low_ref[...] = rows[:, :, JD - 2 :]
    high_ref[...] = rows[:, :, :2]


def vorticity_kernel(
    scale,
    own_ref,
    low_ref,
    high_ref,
    line_ref,
    metric_ref,
    weight_ref,
    stored_ref,
    spectra_ref,
    gram_ref,
    sums_ref,
):
    sums_ref[...] = jnp.zeros_like(sums_ref)
    nf = stored_ref.shape[0]
    xi_x, xi_y, eta_x, eta_y = (metric_ref[i].reshape(JD, 1, P_SIZE) for i in range(4))
    weight = weight_ref[...].reshape(1, JD, 1, P_SIZE)
    twelfth = 1.0 / 12.0

    for f in range(nf):
        new = []
        for r in range(2):
            q = 2 * f + r
            d_x, d_y, d_z = [], [], []
            for c in range(3):
                line = own_ref[q, c].reshape(LD, P_SIZE)
                along = jnp.dot(line, line_ref[...], preferred_element_type=jnp.float32)
                along = (along * twelfth).reshape(JD, NK, P_SIZE)
                center = own_ref[q, c].astype(jnp.float32)
                padded = jnp.concatenate(
                    [
                        low_ref[q, c].astype(jnp.float32),
                        center,
                        high_ref[q, c].astype(jnp.float32),
                    ],
                    axis=0,
                )
                pitch = (
                    padded[:-4] - 8.0 * padded[1:-3] + 8.0 * padded[3:-1] - padded[4:]
                ) * twelfth
                span = (
                    pltpu.roll(center, 2, 1)
                    - 8.0 * pltpu.roll(center, 1, 1)
                    + 8.0 * pltpu.roll(center, NK - 1, 1)
                    - pltpu.roll(center, NK - 2, 1)
                ) * twelfth
                d_x.append(xi_x * along + eta_x * pitch)
                d_y.append(xi_y * along + eta_y * pitch)
                d_z.append(span)
            vort = [d_y[2] - d_z[1], d_z[0] - d_x[2], d_x[1] - d_y[0]]
            vort = [v.astype(jnp.bfloat16) for v in vort]
            for c in range(3):
                spectra_ref[f, r, c] = vort[c]
            new.append(jnp.stack([v.astype(jnp.float32) for v in vort], axis=0))
        columns = [tuple(new)] + [
            tuple(stored_ref[f, a, r].astype(jnp.float32) for r in range(2)) for a in range(2)
        ]

        def put(part, a, b, value):
            total = jnp.sum(value, axis=(0, 1, 2)).reshape(1, P_SIZE)
            total = total[:, :128] + total[:, 128:]
            row = ((f * 2 + part) * 3 + a) * 3 + b
            sums_ref[row : row + 1, :] = total
            if a != b:
                row = ((f * 2 + part) * 3 + b) * 3 + a
                sums_ref[row : row + 1, :] = total if part == 0 else -total

        for a in range(3):
            real, imag = (weight * v for v in columns[a])
            for b in range(a, 3):
                put(0, a, b, real * columns[b][0] + imag * columns[b][1])
                if a != b:
                    put(1, a, b, real * columns[b][1] - imag * columns[b][0])

    total = lax.dot_general(
        jnp.full((8, 128), scale, jnp.float32),
        sums_ref[...],
        (((1,), (1,)), ((), ())),
        precision=lax.Precision.HIGHEST,
        preferred_element_type=jnp.float32,
    )
    gram_ref[...] = jnp.broadcast_to(total[:1].reshape(1, 1, 128), gram_ref.shape)


def shares(snapshots, freq_ids):
    groups = lax.axis_size("block")
    block = lax.axis_index("block")
    held = jnp.transpose(snapshots[0], (0, 1, 3, 2, 4))
    step = held.shape[0] // PARTS
    mine = [held[i * step : (i + 1) * step] for i in range(PARTS)]
    other = [lax.ppermute(v, "block", [(i, i ^ 1) for i in range(groups)]) for v in mine]

    local = held.shape[3]
    both = jnp.stack([block, block ^ 1])[:, None]
    times = (both * local + jnp.arange(local, dtype=jnp.int32)).reshape(-1)
    chips = groups // 2
    target = (block // 2 + jnp.arange(chips, dtype=jnp.int32)) % chips * 2 + block % 2
    ids = jnp.take(freq_ids.reshape(groups, -1), target, axis=0).reshape(-1)
    nq = 2 * NF // groups
    table = fourier_table(ids, times, NT).reshape(2, local, chips, nq)
    table = jnp.transpose(table, (2, 3, 0, 1))
    table = jnp.broadcast_to(table[:, None], (chips, 6, nq, 2, local))
    table = table.reshape(chips, 6 * nq, 2, 1, local)
    row = jnp.arange(6 * nq, dtype=jnp.int32)[:, None, None, None]
    line = jnp.arange(6, dtype=jnp.int32)[:, None]
    table = jnp.where(row // nq == line, table, 0).reshape(chips, 6 * nq, 12 * local)
    pad = ROWS - 6 * nq
    table = jnp.stack(
        [jnp.pad(table, ((0, 0), (0, pad), (0, 0))), jnp.pad(table, ((0, 0), (pad, 0), (0, 0)))]
    ).reshape(2, chips * ROWS, 12 * local)

    operands = []
    for i in range(PARTS):
        own, *sends = pl.pallas_call(
            dft_kernel,
            out_shape=[
                jax.ShapeDtypeStruct(
                    (step // 2, PAIR, P_SIZE), jnp.bfloat16 if k else jnp.float32
                )
                for k in range(chips)
            ],
            in_specs=[VMEM] * 3,
            out_specs=[VMEM] * chips,
            compiler_params=PARAMS,
            name="dft",
        )(mine[i], other[i], table)
        operands.append(own)
        for k, send in enumerate(sends, 1):
            route = [(j, (j + 2 * k) % groups) for j in range(groups)]
            operands.append(lax.ppermute(send, "block", route))
    return pl.pallas_call(
        functools.partial(sum_kernel, PARTS),
        out_shape=jax.ShapeDtypeStruct((held.shape[0], ROWS, P_SIZE), jnp.bfloat16),
        in_specs=[VMEM] * len(operands),
        out_specs=VMEM,
        compiler_params=PARAMS,
        name="sum",
    )(*operands)


def placing(slot_line):
    me = lax.axis_index("space")
    ids = lax.dynamic_index_in_dim(slot_line, me, 1, keepdims=False)
    in_row = jnp.arange(ROWS, dtype=jnp.int32) - (ROWS - 36) * (me % 2)
    held = jnp.where(in_row[None, :] < 18, ids[:, 0:1], ids[:, 1:2])
    inner = in_row % 18
    source = (inner % 6 * 3 + inner // 6)[None, :] * LD + held
    real = (in_row >= 0) & (in_row < 36)
    source = jnp.where((held >= 0) & real[None, :], source, -1).reshape(1, -1)
    target = jnp.arange(18 * LD, dtype=jnp.int32)[:, None]
    return (source == target).astype(jnp.bfloat16)


def per_device(snapshots, slot_line, freq_ids, metrics, weights, stored_spectra):
    groups = lax.axis_size("block")
    holders = lax.axis_size("space")
    velocity = shares(snapshots, freq_ids)
    velocity = lax.all_to_all(velocity, "space", split_axis=0, concat_axis=0, tiled=True)

    nf = NF // groups
    own, low, high = pl.pallas_call(
        place_kernel,
        out_shape=[
            jax.ShapeDtypeStruct((2 * nf, 3, JD, NK, P_SIZE), jnp.bfloat16),
            jax.ShapeDtypeStruct((2 * nf, 3, 2, NK, P_SIZE), jnp.bfloat16),
            jax.ShapeDtypeStruct((2 * nf, 3, 2, NK, P_SIZE), jnp.bfloat16),
        ],
        in_specs=[VMEM, VMEM],
        out_specs=[VMEM, VMEM, VMEM],
        compiler_params=PARAMS,
        name="place",
    )(placing(slot_line), velocity)
    forward = [(i, (i + 1) % holders) for i in range(holders)]
    backward = [(target, source) for source, target in forward]
    low = lax.ppermute(low, "space", forward)
    high = lax.ppermute(high, "space", backward)

    spectra, gram = pl.pallas_call(
        functools.partial(vorticity_kernel, 1.0 / (3.0 * JD * holders * NK * P_SIZE)),
        out_shape=[
            jax.ShapeDtypeStruct((nf, 2, 3, JD, NK, P_SIZE), jnp.bfloat16),
            jax.ShapeDtypeStruct((holders, 1, 128), jnp.float32),
        ],
        in_specs=[VMEM] * 7,
        out_specs=[VMEM, VMEM],
        scratch_shapes=[pltpu.VMEM((128, 128), jnp.float32)],
        compiler_params=PARAMS,
        name="vorticity",
    )(own, low, high, line_matrix(), metrics, weights, stored_spectra)
    gram = lax.all_to_all(gram, "space", split_axis=0, concat_axis=0, tiled=True)
    gram = jnp.sum(gram, axis=(0, 1))[: nf * 18].reshape(nf, 2, 3, 3)
    return (spectra, gram)


def solution(mesh):
    return jax.shard_map(
        per_device,
        mesh=mesh,
        in_specs=(
            P("space", None, None, "block", None, None),
            P(),
            P(),
            P(None, "space", None),
            P("space", None),
            P("block", None, None, None, "space", None, None),
        ),
        out_specs=(P("block", None, None, "space", None, None), P("block", None, None, None)),
        check_vma=False,
    )
```

```python
import functools
import math

import jax
import jax.numpy as jnp
import numpy as np
from jax import lax
from jax.experimental import pallas as pl
from jax.experimental.pallas import tpu as pltpu
from jax.sharding import PartitionSpec as P

P_SIZE = 256
NT = 256
NF = 24
NK = 8
JD = 4
LD = JD * NK
ROWS = 40
PAIR = 72
PARTS = (16, 16)
UNROLL = 2
SHARE_US, JOIN_US = (20, 1), 1
VMEM = pl.BlockSpec(memory_space=pltpu.VMEM)
SMEM = pl.BlockSpec(memory_space=pltpu.SMEM)
PARAMS = pltpu.CompilerParams(vmem_limit_bytes=16 * 1024 * 1024)


def line_matrix():
    d = np.zeros((P_SIZE, P_SIZE), np.float32)
    for p in range(2, P_SIZE - 2):
        d[p - 2, p], d[p - 1, p], d[p + 1, p], d[p + 2, p] = 1, -8, 8, -1
    first, second = (-25, 48, -36, 16, -3), (-3, -10, 18, -6, 1)
    for i in range(5):
        d[i, 0], d[i, 1] = first[i], second[i]
        d[P_SIZE - 1 - i, P_SIZE - 1], d[P_SIZE - 1 - i, P_SIZE - 2] = -first[i], -second[i]
    return jnp.asarray(d, jnp.bfloat16)


def table_kernel(chips, local, block_ref, freq_ref, table_ref):
    block = block_ref[0]
    half = 6 * local
    lane = lax.broadcasted_iota(jnp.int32, (NF, 2 * half), 1)
    far = (lane >= half).astype(jnp.int32)
    time = (block ^ far) * local + ((lane - far * half) & (local - 1))
    row = lax.broadcasted_iota(jnp.int32, (NF, 2 * half), 0)
    freq = jnp.zeros_like(row)
    for f in range(NF):
        freq = jnp.where(row == f, freq_ref[f], freq)
    theta = 2.0 * math.pi / NT * ((time * freq) & (NT - 1)).astype(jnp.float32)
    window = 0.5 - 0.5 * jnp.cos(2.0 * math.pi / NT * time.astype(jnp.float32))
    scale = 1.0 / math.sqrt(0.375 * NT)
    waves = jnp.concatenate(
        [scale * window * jnp.cos(theta), -scale * window * jnp.sin(theta)], axis=0
    ).astype(jnp.bfloat16)

    def line_of(row):
        return sum((row >= 6 * i).astype(jnp.int32) for i in range(1, 6))

    lane = lax.broadcasted_iota(jnp.int32, (ROWS, 2 * half), 1)
    lane_line = line_of((lane - jnp.where(lane >= half, half, 0)) * 6 // local)
    wide = lax.broadcasted_iota(jnp.int32, (ROWS, 2 * half), 0)
    narrow = lax.broadcasted_iota(jnp.int32, (ROWS, 2 * NF), 0)
    wave = lax.broadcasted_iota(jnp.int32, (ROWS, 2 * NF), 1)
    for parity in range(2):
        row = wide - 4 * parity
        kept = (line_of(row) == lane_line) & (row >= 0) & (row < 36)
        row = narrow - 4 * parity
        real = row - 6 * line_of(row)
        for k in range(chips):
            group = ((block >> 1) + k) % chips * 2 + (block & 1)
            pick = wave == group * 3 + (real >> 1) + NF * (real & 1)
            pick = pick.astype(jnp.float32).astype(jnp.bfloat16)
            rows = jnp.dot(pick, waves, preferred_element_type=jnp.float32)
            rows = jnp.where(kept, rows, 0.0).astype(jnp.bfloat16)
            table_ref[parity, k * ROWS : (k + 1) * ROWS] = rows


def share_kernel(mine_ref, other_ref, table_ref, *out_refs):
    def share(d, parity):
        lines = jnp.concatenate(
            [mine_ref[d].reshape(-1, P_SIZE), other_ref[d].reshape(-1, P_SIZE)], axis=0
        )
        return jnp.dot(table_ref[parity], lines, preferred_element_type=jnp.float32)

    def step(pair, carry):
        even, odd = share(2 * pair, 0), share(2 * pair + 1, 1)
        for k, ref in enumerate(out_refs):
            first, second = even[k * ROWS : (k + 1) * ROWS], odd[k * ROWS : (k + 1) * ROWS]
            both = jnp.concatenate(
                [first[: ROWS - 8], first[ROWS - 8 :] + second[:8], second[8:]], axis=0
            )
            ref[pair] = both.astype(ref.dtype)
        return carry

    lax.fori_loop(0, out_refs[0].shape[0], step, 0, unroll=UNROLL)


def join_kernel(kept_ref, passing_ref, out_ref):
    def step(pair, carry):
        total = kept_ref[pair] + passing_ref[pair].astype(jnp.float32)
        out_ref[pair] = total.astype(jnp.bfloat16)
        return carry

    lax.fori_loop(0, out_ref.shape[0], step, 0, unroll=UNROLL)


def sum_kernel(*refs):
    out_ref = refs[-1]
    start = 0
    for part in range(len(refs) // 3):
        own, *rest = refs[3 * part : 3 * part + 3]

        def step(pair, carry, own=own, rest=rest, start=start):
            total = own[pair]
            for ref in rest:
                total = total + ref[pair].astype(jnp.float32)
            total = total.astype(jnp.bfloat16)
            out_ref[start + 2 * pair] = total[:ROWS]
            out_ref[start + 2 * pair + 1] = total[PAIR - ROWS :]
            return carry

        lax.fori_loop(0, own.shape[0], step, 0, unroll=UNROLL)
        start += 2 * own.shape[0]


def place_kernel(place_ref, held_ref, own_ref, low_ref, high_ref):
    held = held_ref[...].reshape(-1, P_SIZE)
    rows = jnp.dot(place_ref[...], held, preferred_element_type=jnp.float32)
    rows = rows.astype(jnp.bfloat16).reshape(own_ref.shape)
    own_ref[...] = rows
    low_ref[...] = rows[:, :, JD - 2 :]
    high_ref[...] = rows[:, :, :2]


def vorticity_kernel(
    scale,
    own_ref,
    low_ref,
    high_ref,
    line_ref,
    metric_ref,
    weight_ref,
    stored_ref,
    spectra_ref,
    gram_ref,
    sums_ref,
):
    sums_ref[...] = jnp.zeros_like(sums_ref)
    nf = stored_ref.shape[0]
    xi_x, xi_y, eta_x, eta_y = (metric_ref[i].reshape(JD, 1, P_SIZE) for i in range(4))
    weight = weight_ref[...].reshape(1, JD, 1, P_SIZE)
    twelfth = 1.0 / 12.0

    for f in range(nf):
        new = []
        for r in range(2):
            q = 2 * f + r
            d_x, d_y, d_z = [], [], []
            for c in range(3):
                line = own_ref[q, c].reshape(LD, P_SIZE)
                along = jnp.dot(line, line_ref[...], preferred_element_type=jnp.float32)
                along = (along * twelfth).reshape(JD, NK, P_SIZE)
                center = own_ref[q, c].astype(jnp.float32)
                padded = jnp.concatenate(
                    [
                        low_ref[q, c].astype(jnp.float32),
                        center,
                        high_ref[q, c].astype(jnp.float32),
                    ],
                    axis=0,
                )
                pitch = (
                    padded[:-4] - 8.0 * padded[1:-3] + 8.0 * padded[3:-1] - padded[4:]
                ) * twelfth
                span = (
                    pltpu.roll(center, 2, 1)
                    - 8.0 * pltpu.roll(center, 1, 1)
                    + 8.0 * pltpu.roll(center, NK - 1, 1)
                    - pltpu.roll(center, NK - 2, 1)
                ) * twelfth
                d_x.append(xi_x * along + eta_x * pitch)
                d_y.append(xi_y * along + eta_y * pitch)
                d_z.append(span)
            vort = [d_y[2] - d_z[1], d_z[0] - d_x[2], d_x[1] - d_y[0]]
            vort = [v.astype(jnp.bfloat16) for v in vort]
            for c in range(3):
                spectra_ref[f, r, c] = vort[c]
            new.append(jnp.stack([v.astype(jnp.float32) for v in vort], axis=0))
        columns = [tuple(new)] + [
            tuple(stored_ref[f, a, r].astype(jnp.float32) for r in range(2)) for a in range(2)
        ]

        def put(part, a, b, value):
            total = jnp.sum(value, axis=(0, 1, 2)).reshape(1, P_SIZE)
            total = total[:, :128] + total[:, 128:]
            row = ((f * 2 + part) * 3 + a) * 3 + b
            sums_ref[row : row + 1, :] = total
            if a != b:
                row = ((f * 2 + part) * 3 + b) * 3 + a
                sums_ref[row : row + 1, :] = total if part == 0 else -total

        for a in range(3):
            real, imag = (weight * v for v in columns[a])
            for b in range(a, 3):
                put(0, a, b, real * columns[b][0] + imag * columns[b][1])
                if a != b:
                    put(1, a, b, real * columns[b][1] - imag * columns[b][0])

    total = lax.dot_general(
        jnp.full((8, 128), scale, jnp.float32),
        sums_ref[...],
        (((1,), (1,)), ((), ())),
        precision=lax.Precision.HIGHEST,
        preferred_element_type=jnp.float32,
    )
    gram_ref[...] = jnp.broadcast_to(total[:1].reshape(1, 1, 128), gram_ref.shape)


def cost(us):
    return pl.CostEstimate(flops=int(us * 1e9), bytes_accessed=0, transcendentals=0)


def shares(snapshots, freq_ids):
    groups = lax.axis_size("block")
    chips = groups // 2
    block = lax.axis_index("block")
    held = jnp.transpose(snapshots[0], (0, 1, 3, 2, 4))
    owners, _, _, local, _ = held.shape

    def along(value, k):
        route = [(j, (j + 2 * k) % groups) for j in range(groups)]
        return lax.ppermute(value, "block", route)

    table = pl.pallas_call(
        functools.partial(table_kernel, chips, local),
        out_shape=jax.ShapeDtypeStruct((2, chips * ROWS, 12 * local), jnp.bfloat16),
        in_specs=[SMEM, SMEM],
        out_specs=VMEM,
        compiler_params=PARAMS,
        name="table",
    )(block.reshape(1), freq_ids)
    lines, start = [], 0
    for step in PARTS:
        mine = held[start : start + step]
        if start:
            mine, table = lax.optimization_barrier((mine, table))
        lines.append((mine, lax.ppermute(mine, "block", [(i, i ^ 1) for i in range(groups)])))
        start += step

    operands, previous = [], None
    for part, (mine, other) in enumerate(lines):
        direct, joined = ((chips - 1, 1), (1, chips - 1))[part]
        if part:
            other, previous = lax.optimization_barrier((other, previous))
        shape = (mine.shape[0] // 2, PAIR, P_SIZE)
        results = pl.pallas_call(
            share_kernel,
            out_shape=[
                jax.ShapeDtypeStruct(shape, jnp.float32 if k in (0, joined) else jnp.bfloat16)
                for k in range(chips)
            ],
            in_specs=[VMEM] * 3,
            out_specs=[VMEM] * chips,
            compiler_params=PARAMS,
            cost_estimate=cost(SHARE_US[part]),
            name="share",
        )(mine, other, table)
        previous = results[0]
        passing = along(results[2], joined)
        sent = along(results[direct], direct)
        if part:
            passing, operands[1] = lax.optimization_barrier((passing, operands[1]))
        else:
            passing, sent = lax.optimization_barrier((passing, sent))
        total = pl.pallas_call(
            join_kernel,
            out_shape=jax.ShapeDtypeStruct(shape, jnp.bfloat16),
            in_specs=[VMEM] * 2,
            out_specs=VMEM,
            compiler_params=PARAMS,
            cost_estimate=cost(JOIN_US),
            name="join",
        )(results[joined], passing)
        operands += [results[0], sent, along(total, joined)]
    return pl.pallas_call(
        sum_kernel,
        out_shape=jax.ShapeDtypeStruct((owners, ROWS, P_SIZE), jnp.bfloat16),
        in_specs=[VMEM] * len(operands),
        out_specs=VMEM,
        compiler_params=PARAMS,
        name="sum",
    )(*operands)


def placing(slot_line):
    me = lax.axis_index("space")
    ids = lax.dynamic_index_in_dim(slot_line, me, 1, keepdims=False)
    in_row = jnp.arange(ROWS, dtype=jnp.int32) - (ROWS - 36) * (me % 2)
    held = jnp.where(in_row[None, :] < 18, ids[:, 0:1], ids[:, 1:2])
    inner = in_row % 18
    source = (inner % 6 * 3 + inner // 6)[None, :] * LD + held
    real = (in_row >= 0) & (in_row < 36)
    source = jnp.where((held >= 0) & real[None, :], source, -1).reshape(1, -1)
    target = jnp.arange(18 * LD, dtype=jnp.int32)[:, None]
    return (source == target).astype(jnp.bfloat16)


def per_device(snapshots, slot_line, freq_ids, metrics, weights, stored_spectra):
    groups = lax.axis_size("block")
    holders = lax.axis_size("space")
    velocity = shares(snapshots, freq_ids)
    velocity = lax.all_to_all(velocity, "space", split_axis=0, concat_axis=0, tiled=True)

    nf = NF // groups
    own, low, high = pl.pallas_call(
        place_kernel,
        out_shape=[
            jax.ShapeDtypeStruct((2 * nf, 3, JD, NK, P_SIZE), jnp.bfloat16),
            jax.ShapeDtypeStruct((2 * nf, 3, 2, NK, P_SIZE), jnp.bfloat16),
            jax.ShapeDtypeStruct((2 * nf, 3, 2, NK, P_SIZE), jnp.bfloat16),
        ],
        in_specs=[VMEM, VMEM],
        out_specs=[VMEM, VMEM, VMEM],
        compiler_params=PARAMS,
        name="place",
    )(placing(slot_line), velocity)
    forward = [(i, (i + 1) % holders) for i in range(holders)]
    backward = [(target, source) for source, target in forward]
    low = lax.ppermute(low, "space", forward)
    high = lax.ppermute(high, "space", backward)

    spectra, gram = pl.pallas_call(
        functools.partial(vorticity_kernel, 1.0 / (3.0 * JD * holders * NK * P_SIZE)),
        out_shape=[
            jax.ShapeDtypeStruct((nf, 2, 3, JD, NK, P_SIZE), jnp.bfloat16),
            jax.ShapeDtypeStruct((holders, 1, 128), jnp.float32),
        ],
        in_specs=[VMEM] * 7,
        out_specs=[VMEM, VMEM],
        scratch_shapes=[pltpu.VMEM((128, 128), jnp.float32)],
        compiler_params=PARAMS,
        name="vorticity",
    )(own, low, high, line_matrix(), metrics, weights, stored_spectra)
    gram = lax.all_to_all(gram, "space", split_axis=0, concat_axis=0, tiled=True)
    gram = jnp.sum(gram, axis=(0, 1))[: nf * 18].reshape(nf, 2, 3, 3)
    return (spectra, gram)


def solution(mesh):
    return jax.shard_map(
        per_device,
        mesh=mesh,
        in_specs=(
            P("space", None, None, "block", None, None),
            P(),
            P(),
            P(None, "space", None),
            P("space", None),
            P("block", None, None, None, "space", None, None),
        ),
        out_specs=(P("block", None, None, "space", None, None), P("block", None, None, None)),
        check_vma=False,
    )
```

```python
import functools
import math

import jax
import jax.numpy as jnp
import numpy as np
from jax import lax
from jax.experimental import pallas as pl
from jax.experimental.pallas import tpu as pltpu
from jax.sharding import PartitionSpec as P

P_SIZE = 256
NT = 256
NF = 24
NK = 8
JD = 4
LD = JD * NK
ROWS = 40
PAIR = 72
PARTS = (16, 16)
SHARE_US, JOIN_US, SUM_US = (20, 1), 1, (20, 1)
VMEM = pl.BlockSpec(memory_space=pltpu.VMEM)
SMEM = pl.BlockSpec(memory_space=pltpu.SMEM)
ANY = pl.BlockSpec(memory_space=pl.ANY)
HBM = pl.BlockSpec(memory_space=pltpu.HBM)
FETCHES = 4
PARAMS = pltpu.CompilerParams(vmem_limit_bytes=16 * 1024 * 1024)


def line_matrix():
    d = np.zeros((P_SIZE, P_SIZE), np.float32)
    for p in range(2, P_SIZE - 2):
        d[p - 2, p], d[p - 1, p], d[p + 1, p], d[p + 2, p] = 1, -8, 8, -1
    first, second = (-25, 48, -36, 16, -3), (-3, -10, 18, -6, 1)
    for i in range(5):
        d[i, 0], d[i, 1] = first[i], second[i]
        d[P_SIZE - 1 - i, P_SIZE - 1], d[P_SIZE - 1 - i, P_SIZE - 2] = -first[i], -second[i]
    return jnp.asarray(d, jnp.bfloat16)


def table_kernel(chips, local, block_ref, freq_ref, table_ref):
    block = block_ref[0]
    half = 6 * local
    lane = lax.broadcasted_iota(jnp.int32, (NF, 2 * half), 1)
    far = (lane >= half).astype(jnp.int32)
    time = (block ^ far) * local + ((lane - far * half) & (local - 1))
    row = lax.broadcasted_iota(jnp.int32, (NF, 2 * half), 0)
    freq = jnp.zeros_like(row)
    for f in range(NF):
        freq = jnp.where(row == f, freq_ref[f], freq)
    theta = 2.0 * math.pi / NT * ((time * freq) & (NT - 1)).astype(jnp.float32)
    window = 0.5 - 0.5 * jnp.cos(2.0 * math.pi / NT * time.astype(jnp.float32))
    scale = 1.0 / math.sqrt(0.375 * NT)
    waves = jnp.concatenate(
        [scale * window * jnp.cos(theta), -scale * window * jnp.sin(theta)], axis=0
    ).astype(jnp.bfloat16)

    def line_of(row):
        return sum((row >= 6 * i).astype(jnp.int32) for i in range(1, 6))

    lane = lax.broadcasted_iota(jnp.int32, (ROWS, 2 * half), 1)
    lane_line = line_of((lane - jnp.where(lane >= half, half, 0)) * 6 // local)
    wide = lax.broadcasted_iota(jnp.int32, (ROWS, 2 * half), 0)
    narrow = lax.broadcasted_iota(jnp.int32, (ROWS, 2 * NF), 0)
    wave = lax.broadcasted_iota(jnp.int32, (ROWS, 2 * NF), 1)
    for parity in range(2):
        row = wide - 4 * parity
        kept = (line_of(row) == lane_line) & (row >= 0) & (row < 36)
        row = narrow - 4 * parity
        real = row - 6 * line_of(row)
        for k in range(chips):
            group = ((block >> 1) + k) % chips * 2 + (block & 1)
            pick = wave == group * 3 + (real >> 1) + NF * (real & 1)
            pick = pick.astype(jnp.float32).astype(jnp.bfloat16)
            rows = jnp.dot(pick, waves, preferred_element_type=jnp.float32)
            rows = jnp.where(kept, rows, 0.0).astype(jnp.bfloat16)
            table_ref[parity, k * ROWS : (k + 1) * ROWS] = rows


def share_kernel(mine_ref, other_ref, table_ref, *refs):
    *out_refs, fetched_ref, sems = refs

    def share(d, parity):
        lines = jnp.concatenate(
            [mine_ref[d].reshape(-1, P_SIZE), fetched_ref[d].reshape(-1, P_SIZE)], axis=0
        )
        return jnp.dot(table_ref[parity], lines, preferred_element_type=jnp.float32)

    def step(pair, carry):
        even, odd = share(2 * pair, 0), share(2 * pair + 1, 1)
        for k, ref in enumerate(out_refs):
            first, second = even[k * ROWS : (k + 1) * ROWS], odd[k * ROWS : (k + 1) * ROWS]
            both = jnp.concatenate(
                [first[: ROWS - 8], first[ROWS - 8 :] + second[:8], second[8:]], axis=0
            )
            ref[pair] = both.astype(ref.dtype)
        return carry

    pairs = out_refs[0].shape[0]
    ends = [pairs * (i + 1) // FETCHES for i in range(FETCHES)]
    copies = []
    for i, (start, end) in enumerate(zip([0] + ends, ends)):
        owners = pl.ds(2 * start, 2 * (end - start))
        copies.append(
            pltpu.make_async_copy(other_ref.at[owners], fetched_ref.at[owners], sems.at[i])
        )
        copies[-1].start()
    for copy, start, end in zip(copies, [0] + ends, ends):
        copy.wait()
        lax.fori_loop(start, end, step, 0, unroll=2)


def join_kernel(kept_ref, passing_ref, *refs):
    out_ref = refs[-1]

    def step(pair, carry):
        total = kept_ref[pair] + passing_ref[pair].astype(jnp.float32)
        out_ref[pair] = total.astype(jnp.bfloat16)
        return carry

    lax.fori_loop(0, out_ref.shape[0], step, 0)


def sum_kernel(own_ref, sent_ref, joined_ref, *refs):
    *before_refs, out_ref = refs
    start = 0
    for before_ref in before_refs:
        start = before_ref.shape[0]
        out_ref[:start] = before_ref[...]

    def step(pair, carry):
        total = own_ref[pair] + sent_ref[pair].astype(jnp.float32)
        total = (total + joined_ref[pair].astype(jnp.float32)).astype(jnp.bfloat16)
        out_ref[start + 2 * pair] = total[:ROWS]
        out_ref[start + 2 * pair + 1] = total[PAIR - ROWS :]
        return carry

    lax.fori_loop(0, own_ref.shape[0], step, 0)


def place_kernel(place_ref, held_ref, own_ref, low_ref, high_ref):
    held = held_ref[...].reshape(-1, P_SIZE)
    rows = jnp.dot(place_ref[...], held, preferred_element_type=jnp.float32)
    rows = rows.astype(jnp.bfloat16).reshape(own_ref.shape)
    own_ref[...] = rows
    low_ref[...] = rows[:, :, JD - 2 :]
    high_ref[...] = rows[:, :, :2]


def add_products(sums_ref, f, a, b, left, right):
    def put(part, value):
        total = jnp.sum(value, axis=(0, 1, 2)).reshape(1, P_SIZE)
        total = total[:, :128] + total[:, 128:]
        row = ((f * 2 + part) * 3 + a) * 3 + b
        sums_ref[row : row + 1, :] = total
        if a != b:
            row = ((f * 2 + part) * 3 + b) * 3 + a
            sums_ref[row : row + 1, :] = total if part == 0 else -total

    put(0, left[0] * right[0] + left[1] * right[1])
    if a != b:
        put(1, left[0] * right[1] - left[1] * right[0])


def column(ref, f, a):
    return tuple(ref[f, a, r].astype(jnp.float32) for r in range(2))


def stored_kernel(weight_ref, stored_ref, sums_ref):
    sums_ref[...] = jnp.zeros_like(sums_ref)
    weight = weight_ref[...].reshape(1, JD, 1, P_SIZE)
    for f in range(stored_ref.shape[0]):
        columns = [column(stored_ref, f, a) for a in range(2)]
        for a in range(2):
            left = tuple(weight * v for v in columns[a])
            for b in range(a, 2):
                add_products(sums_ref, f, a + 1, b + 1, left, columns[b])


def within_kernel(own_ref, line_ref, metric_ref, base_ref):
    xi_x, xi_y = (metric_ref[i].reshape(JD, 1, P_SIZE) for i in range(2))
    twelfth = 1.0 / 12.0
    for q in range(own_ref.shape[0]):
        along, span = [], []
        for c in range(3):
            line = own_ref[q, c].reshape(LD, P_SIZE)
            value = jnp.dot(line, line_ref[...], preferred_element_type=jnp.float32)
            along.append((value * twelfth).reshape(JD, NK, P_SIZE))
        for c in range(2):
            center = own_ref[q, c].astype(jnp.float32)
            value = (
                pltpu.roll(center, 2, 1)
                - 8.0 * pltpu.roll(center, 1, 1)
                + 8.0 * pltpu.roll(center, NK - 1, 1)
                - pltpu.roll(center, NK - 2, 1)
            )
            span.append(value * twelfth)
        base_ref[q, 0] = xi_y * along[2] - span[1]
        base_ref[q, 1] = span[0] - xi_x * along[2]
        base_ref[q, 2] = xi_x * along[1] - xi_y * along[0]


def vorticity_kernel(
    scale,
    own_ref,
    low_ref,
    high_ref,
    base_ref,
    metric_ref,
    weight_ref,
    stored_ref,
    before_ref,
    spectra_ref,
    gram_ref,
    sums_ref,
):
    sums_ref[...] = before_ref[...]
    eta_x, eta_y = (metric_ref[i].reshape(JD, 1, P_SIZE) * (1.0 / 12.0) for i in (2, 3))
    weight = weight_ref[...].reshape(1, JD, 1, P_SIZE)
    for f in range(stored_ref.shape[0]):
        new = []
        for r in range(2):
            q = 2 * f + r
            pitch = []
            for c in range(3):
                padded = jnp.concatenate(
                    [ref[q, c].astype(jnp.float32) for ref in (low_ref, own_ref, high_ref)],
                    axis=0,
                )
                pitch.append(padded[:-4] - 8.0 * padded[1:-3] + 8.0 * padded[3:-1] - padded[4:])
            vort = [
                base_ref[q, 0] + eta_y * pitch[2],
                base_ref[q, 1] - eta_x * pitch[2],
                base_ref[q, 2] + eta_x * pitch[1] - eta_y * pitch[0],
            ]
            vort = [v.astype(jnp.bfloat16) for v in vort]
            for c in range(3):
                spectra_ref[f, r, c] = vort[c]
            new.append(jnp.stack([v.astype(jnp.float32) for v in vort], axis=0))
        left = tuple(weight * v for v in new)
        add_products(sums_ref, f, 0, 0, left, new)
        for a in range(2):
            add_products(sums_ref, f, 0, a + 1, left, column(stored_ref, f, a))

    total = lax.dot_general(
        jnp.full((8, 128), scale, jnp.float32),
        sums_ref[...],
        (((1,), (1,)), ((), ())),
        precision=lax.Precision.HIGHEST,
        preferred_element_type=jnp.float32,
    )
    gram_ref[...] = jnp.broadcast_to(total[:1].reshape(1, 1, 128), gram_ref.shape)


def cost(us):
    return pl.CostEstimate(flops=int(us * 1e9), bytes_accessed=0, transcendentals=0)


def shares(snapshots, freq_ids):
    groups = lax.axis_size("block")
    chips = groups // 2
    block = lax.axis_index("block")
    held = jnp.transpose(snapshots[0], (0, 1, 3, 2, 4))
    owners, _, _, local, _ = held.shape

    def along(value, k):
        route = [(j, (j + 2 * k) % groups) for j in range(groups)]
        return lax.ppermute(value, "block", route)

    table = pl.pallas_call(
        functools.partial(table_kernel, chips, local),
        out_shape=jax.ShapeDtypeStruct((2, chips * ROWS, 12 * local), jnp.bfloat16),
        in_specs=[SMEM, SMEM],
        out_specs=VMEM,
        compiler_params=PARAMS,
        name="table",
    )(block.reshape(1), freq_ids)
    lines, start = [], 0
    for step in PARTS:
        if start:
            held, table = lax.optimization_barrier((held, table))
        mine = held[start : start + step]
        lines.append((mine, lax.ppermute(mine, "block", [(i, i ^ 1) for i in range(groups)])))
        start += step

    total, previous, passed = None, None, []
    for part, (mine, other) in enumerate(lines):
        direct, joined = ((chips - 1, 1), (1, chips - 1))[part]
        if part:
            other, previous = lax.optimization_barrier((other, previous))
        shape = (mine.shape[0] // 2, PAIR, P_SIZE)
        results = pl.pallas_call(
            share_kernel,
            out_shape=[
                jax.ShapeDtypeStruct(shape, jnp.float32 if k in (0, joined) else jnp.bfloat16)
                for k in range(chips)
            ],
            in_specs=[VMEM, HBM, VMEM],
            out_specs=[VMEM] * chips,
            scratch_shapes=[
                pltpu.VMEM(mine.shape, jnp.bfloat16),
                pltpu.SemaphoreType.DMA((FETCHES,)),
            ],
            compiler_params=PARAMS,
            cost_estimate=cost(SHARE_US[part]),
            name="share",
        )(mine, other, table)
        previous = results[0]
        passing = along(results[2], joined)
        sent = along(results[direct], direct)
        if part:
            earlier = [total]
        else:
            earlier = []
        passing, sent = lax.optimization_barrier((passing, sent))
        total = pl.pallas_call(
            join_kernel,
            out_shape=jax.ShapeDtypeStruct(shape, jnp.bfloat16),
            in_specs=[VMEM] * 2 + [ANY] * len(earlier),
            out_specs=VMEM,
            compiler_params=PARAMS,
            cost_estimate=cost(JOIN_US),
            name="join",
        )(results[joined], passing, *earlier)
        passed.append((results[0], sent, along(total, joined)))
    velocity = []
    for part, operands in enumerate(passed):
        velocity = [
            pl.pallas_call(
                sum_kernel,
                out_shape=jax.ShapeDtypeStruct(
                    (sum(PARTS[: part + 1]), ROWS, P_SIZE), jnp.bfloat16
                ),
                in_specs=[VMEM] * (3 + part),
                out_specs=VMEM,
                compiler_params=PARAMS,
                cost_estimate=cost(SUM_US[part]),
                name="sum",
            )(*operands, *velocity)
        ]
    return velocity[0]


def placing(slot_line):
    me = lax.axis_index("space")
    ids = lax.dynamic_index_in_dim(slot_line, me, 1, keepdims=False)
    in_row = jnp.arange(ROWS, dtype=jnp.int32) - (ROWS - 36) * (me % 2)
    held = jnp.where(in_row[None, :] < 18, ids[:, 0:1], ids[:, 1:2])
    inner = in_row % 18
    source = (inner % 6 * 3 + inner // 6)[None, :] * LD + held
    real = (in_row >= 0) & (in_row < 36)
    source = jnp.where((held >= 0) & real[None, :], source, -1).reshape(1, -1)
    target = jnp.arange(18 * LD, dtype=jnp.int32)[:, None]
    return (source == target).astype(jnp.bfloat16)


def per_device(snapshots, slot_line, freq_ids, metrics, weights, stored_spectra):
    groups = lax.axis_size("block")
    holders = lax.axis_size("space")
    velocity = shares(snapshots, freq_ids)
    velocity = lax.all_to_all(velocity, "space", split_axis=0, concat_axis=0, tiled=True)

    nf = NF // groups
    own, low, high = pl.pallas_call(
        place_kernel,
        out_shape=[
            jax.ShapeDtypeStruct((2 * nf, 3, JD, NK, P_SIZE), jnp.bfloat16),
            jax.ShapeDtypeStruct((2 * nf, 3, 2, NK, P_SIZE), jnp.bfloat16),
            jax.ShapeDtypeStruct((2 * nf, 3, 2, NK, P_SIZE), jnp.bfloat16),
        ],
        in_specs=[VMEM, VMEM],
        out_specs=[VMEM, VMEM, VMEM],
        compiler_params=PARAMS,
        name="place",
    )(placing(slot_line), velocity)
    forward = [(i, (i + 1) % holders) for i in range(holders)]
    backward = [(target, source) for source, target in forward]
    low = lax.ppermute(low, "space", forward)
    high = lax.ppermute(high, "space", backward)
    base = pl.pallas_call(
        within_kernel,
        out_shape=jax.ShapeDtypeStruct((2 * nf, 3, JD, NK, P_SIZE), jnp.float32),
        in_specs=[VMEM] * 3,
        out_specs=VMEM,
        compiler_params=PARAMS,
        cost_estimate=cost(5),
        name="within",
    )(own, line_matrix(), metrics)
    before = pl.pallas_call(
        stored_kernel,
        out_shape=jax.ShapeDtypeStruct((128, 128), jnp.float32),
        in_specs=[VMEM] * 2,
        out_specs=VMEM,
        compiler_params=PARAMS,
        cost_estimate=cost(1),
        name="stored",
    )(weights, stored_spectra)

    spectra, gram = pl.pallas_call(
        functools.partial(vorticity_kernel, 1.0 / (3.0 * JD * holders * NK * P_SIZE)),
        out_shape=[
            jax.ShapeDtypeStruct((nf, 2, 3, JD, NK, P_SIZE), jnp.bfloat16),
            jax.ShapeDtypeStruct((holders, 1, 128), jnp.float32),
        ],
        in_specs=[VMEM] * 8,
        out_specs=[VMEM, VMEM],
        scratch_shapes=[pltpu.VMEM((128, 128), jnp.float32)],
        compiler_params=PARAMS,
        name="vorticity",
    )(own, low, high, base, metrics, weights, stored_spectra, before)
    gram = lax.all_to_all(gram, "space", split_axis=0, concat_axis=0, tiled=True)
    gram = jnp.sum(gram, axis=(0, 1))[: nf * 18].reshape(nf, 2, 3, 3)
    return (spectra, gram)


def solution(mesh):
    return jax.shard_map(
        per_device,
        mesh=mesh,
        in_specs=(
            P("space", None, None, "block", None, None),
            P(),
            P(),
            P(None, "space", None),
            P("space", None),
            P("block", None, None, None, "space", None, None),
        ),
        out_specs=(P("block", None, None, "space", None, None), P("block", None, None, None)),
        check_vma=False,
    )
```

```python
import functools
import math

import jax
import jax.numpy as jnp
import numpy as np
from jax import lax
from jax.experimental import pallas as pl
from jax.experimental.pallas import tpu as pltpu
from jax.sharding import PartitionSpec as P

P_SIZE = 256
NT = 256
NF = 24
NK = 8
JD = 4
LD = JD * NK
ROWS = 40
PAIR = 72
PARTS = (18, 14)
SHARE_US, JOIN_US, SUM_US = (20, 1), 1, (20, 1)
VMEM = pl.BlockSpec(memory_space=pltpu.VMEM)
SMEM = pl.BlockSpec(memory_space=pltpu.SMEM)
ANY = pl.BlockSpec(memory_space=pl.ANY)
HBM = pl.BlockSpec(memory_space=pltpu.HBM)
FETCHES = 4
PARAMS = pltpu.CompilerParams(vmem_limit_bytes=16 * 1024 * 1024)


def line_matrix():
    d = np.zeros((P_SIZE, P_SIZE), np.float32)
    for p in range(2, P_SIZE - 2):
        d[p - 2, p], d[p - 1, p], d[p + 1, p], d[p + 2, p] = 1, -8, 8, -1
    first, second = (-25, 48, -36, 16, -3), (-3, -10, 18, -6, 1)
    for i in range(5):
        d[i, 0], d[i, 1] = first[i], second[i]
        d[P_SIZE - 1 - i, P_SIZE - 1], d[P_SIZE - 1 - i, P_SIZE - 2] = -first[i], -second[i]
    return jnp.asarray(d, jnp.bfloat16)


def table_kernel(chips, local, block_ref, freq_ref, table_ref):
    block = block_ref[0]
    half = 6 * local
    lane = lax.broadcasted_iota(jnp.int32, (NF, 2 * half), 1)
    far = (lane >= half).astype(jnp.int32)
    time = (block ^ far) * local + ((lane - far * half) & (local - 1))
    row = lax.broadcasted_iota(jnp.int32, (NF, 2 * half), 0)
    freq = jnp.zeros_like(row)
    for f in range(NF):
        freq = jnp.where(row == f, freq_ref[f], freq)
    theta = 2.0 * math.pi / NT * ((time * freq) & (NT - 1)).astype(jnp.float32)
    window = 0.5 - 0.5 * jnp.cos(2.0 * math.pi / NT * time.astype(jnp.float32))
    scale = 1.0 / math.sqrt(0.375 * NT)
    waves = jnp.concatenate(
        [scale * window * jnp.cos(theta), -scale * window * jnp.sin(theta)], axis=0
    ).astype(jnp.bfloat16)

    def line_of(row):
        return sum((row >= 6 * i).astype(jnp.int32) for i in range(1, 6))

    lane = lax.broadcasted_iota(jnp.int32, (ROWS, 2 * half), 1)
    lane_line = line_of((lane - jnp.where(lane >= half, half, 0)) * 6 // local)
    wide = lax.broadcasted_iota(jnp.int32, (ROWS, 2 * half), 0)
    narrow = lax.broadcasted_iota(jnp.int32, (ROWS, 2 * NF), 0)
    wave = lax.broadcasted_iota(jnp.int32, (ROWS, 2 * NF), 1)
    for parity in range(2):
        row = wide - 4 * parity
        kept = (line_of(row) == lane_line) & (row >= 0) & (row < 36)
        row = narrow - 4 * parity
        real = row - 6 * line_of(row)
        for k in range(chips):
            group = ((block >> 1) + k) % chips * 2 + (block & 1)
            pick = wave == group * 3 + (real >> 1) + NF * (real & 1)
            pick = pick.astype(jnp.float32).astype(jnp.bfloat16)
            rows = jnp.dot(pick, waves, preferred_element_type=jnp.float32)
            rows = jnp.where(kept, rows, 0.0).astype(jnp.bfloat16)
            table_ref[parity, k * ROWS : (k + 1) * ROWS] = rows


def share_kernel(mine_ref, other_ref, table_ref, *refs):
    *out_refs, fetched_ref, sems = refs

    def share(d, parity):
        lines = jnp.concatenate(
            [mine_ref[d].reshape(-1, P_SIZE), fetched_ref[d].reshape(-1, P_SIZE)], axis=0
        )
        return jnp.dot(table_ref[parity], lines, preferred_element_type=jnp.float32)

    def step(pair, carry):
        even, odd = share(2 * pair, 0), share(2 * pair + 1, 1)
        for k, ref in enumerate(out_refs):
            first, second = even[k * ROWS : (k + 1) * ROWS], odd[k * ROWS : (k + 1) * ROWS]
            both = jnp.concatenate(
                [first[: ROWS - 8], first[ROWS - 8 :] + second[:8], second[8:]], axis=0
            )
            ref[pair] = both.astype(ref.dtype)
        return carry

    pairs = out_refs[0].shape[0]
    ends = [pairs * (i + 1) // FETCHES for i in range(FETCHES)]
    copies = []
    for i, (start, end) in enumerate(zip([0] + ends, ends)):
        owners = pl.ds(2 * start, 2 * (end - start))
        copies.append(
            pltpu.make_async_copy(other_ref.at[owners], fetched_ref.at[owners], sems.at[i])
        )
        copies[-1].start()
    for copy, start, end in zip(copies, [0] + ends, ends):
        copy.wait()
        lax.fori_loop(start, end, step, 0, unroll=2)


def join_kernel(kept_ref, passing_ref, *refs):
    out_ref = refs[-1]

    def step(pair, carry):
        total = kept_ref[pair] + passing_ref[pair].astype(jnp.float32)
        out_ref[pair] = total.astype(jnp.bfloat16)
        return carry

    lax.fori_loop(0, out_ref.shape[0], step, 0)


def sum_kernel(own_ref, sent_ref, joined_ref, *refs):
    *before_refs, out_ref = refs
    start = 0
    for before_ref in before_refs:
        start = before_ref.shape[0]
        out_ref[:start] = before_ref[...]
    low = lax.broadcasted_iota(jnp.int32, (8, 128), 0) < 4

    def step(pair, carry):
        total = own_ref[pair] + sent_ref[pair].astype(jnp.float32)
        total = total + joined_ref[pair].astype(jnp.float32)
        left, right = total[:, :128], total[:, 128:]
        middle = slice(32, 40)
        even = jnp.where(low, left[middle], pltpu.roll(right[middle], 4, 0))
        odd = jnp.where(low, pltpu.roll(left[middle], 4, 0), right[middle])
        for i, mixed, rows in ((0, even, slice(0, 32)), (1, odd, slice(40, 72))):
            block = jnp.concatenate([left[rows], mixed, right[rows]], axis=0)
            out_ref[start + 2 * pair + i] = block.astype(jnp.bfloat16)
        return carry

    lax.fori_loop(0, own_ref.shape[0], step, 0)


def place_kernel(place_ref, packed_ref, own_ref, low_ref, high_ref, held_ref):
    def unpack(h, carry):
        mixed = packed_ref[h, 32:40].astype(jnp.float32)
        turned = pltpu.roll(mixed, 4, 0).astype(jnp.bfloat16)
        held_ref[h, :, :128] = packed_ref[h, :40]
        held_ref[h, :, 128:] = jnp.concatenate([packed_ref[h, 40:], turned], axis=0)
        return carry

    lax.fori_loop(0, packed_ref.shape[0], unpack, 0, unroll=2)
    held = held_ref[...].reshape(-1, P_SIZE)
    rows = jnp.dot(place_ref[...], held, preferred_element_type=jnp.float32)
    rows = rows.astype(jnp.bfloat16).reshape(own_ref.shape)
    own_ref[...] = rows
    low_ref[...] = rows[:, :, JD - 2 :]
    high_ref[...] = rows[:, :, :2]


def add_products(sums_ref, f, a, b, left, right):
    def put(part, value):
        total = jnp.sum(value, axis=(0, 1, 2)).reshape(1, P_SIZE)
        total = total[:, :128] + total[:, 128:]
        row = ((f * 2 + part) * 3 + a) * 3 + b
        sums_ref[row : row + 1, :] = total
        if a != b:
            row = ((f * 2 + part) * 3 + b) * 3 + a
            sums_ref[row : row + 1, :] = total if part == 0 else -total

    put(0, left[0] * right[0] + left[1] * right[1])
    if a != b:
        put(1, left[0] * right[1] - left[1] * right[0])


def column(ref, f, a):
    return tuple(ref[f, a, r].astype(jnp.float32) for r in range(2))


def stored_kernel(weight_ref, stored_ref, sums_ref):
    sums_ref[...] = jnp.zeros_like(sums_ref)
    weight = weight_ref[...].reshape(1, JD, 1, P_SIZE)
    for f in range(stored_ref.shape[0]):
        columns = [column(stored_ref, f, a) for a in range(2)]
        for a in range(2):
            left = tuple(weight * v for v in columns[a])
            for b in range(a, 2):
                add_products(sums_ref, f, a + 1, b + 1, left, columns[b])


def within_kernel(own_ref, line_ref, metric_ref, base_ref):
    xi_x, xi_y = (metric_ref[i].reshape(JD, 1, P_SIZE) for i in range(2))
    twelfth = 1.0 / 12.0
    for q in range(own_ref.shape[0]):
        along, span = [], []
        for c in range(3):
            line = own_ref[q, c].reshape(LD, P_SIZE)
            value = jnp.dot(line, line_ref[...], preferred_element_type=jnp.float32)
            along.append((value * twelfth).reshape(JD, NK, P_SIZE))
        for c in range(2):
            center = own_ref[q, c].astype(jnp.float32)
            value = (
                pltpu.roll(center, 2, 1)
                - 8.0 * pltpu.roll(center, 1, 1)
                + 8.0 * pltpu.roll(center, NK - 1, 1)
                - pltpu.roll(center, NK - 2, 1)
            )
            span.append(value * twelfth)
        base_ref[q, 0] = xi_y * along[2] - span[1]
        base_ref[q, 1] = span[0] - xi_x * along[2]
        base_ref[q, 2] = xi_x * along[1] - xi_y * along[0]


def vorticity_kernel(
    scale,
    own_ref,
    low_ref,
    high_ref,
    base_ref,
    metric_ref,
    weight_ref,
    stored_ref,
    before_ref,
    spectra_ref,
    gram_ref,
    sums_ref,
):
    sums_ref[...] = before_ref[...]
    eta_x, eta_y = (metric_ref[i].reshape(JD, 1, P_SIZE) * (1.0 / 12.0) for i in (2, 3))
    weight = weight_ref[...].reshape(1, JD, 1, P_SIZE)
    for f in range(stored_ref.shape[0]):
        new = []
        for r in range(2):
            q = 2 * f + r
            pitch = []
            for c in range(3):
                padded = jnp.concatenate(
                    [ref[q, c].astype(jnp.float32) for ref in (low_ref, own_ref, high_ref)],
                    axis=0,
                )
                pitch.append(padded[:-4] - 8.0 * padded[1:-3] + 8.0 * padded[3:-1] - padded[4:])
            vort = [
                base_ref[q, 0] + eta_y * pitch[2],
                base_ref[q, 1] - eta_x * pitch[2],
                base_ref[q, 2] + eta_x * pitch[1] - eta_y * pitch[0],
            ]
            vort = [v.astype(jnp.bfloat16) for v in vort]
            for c in range(3):
                spectra_ref[f, r, c] = vort[c]
            new.append(jnp.stack([v.astype(jnp.float32) for v in vort], axis=0))
        left = tuple(weight * v for v in new)
        add_products(sums_ref, f, 0, 0, left, new)
        for a in range(2):
            add_products(sums_ref, f, 0, a + 1, left, column(stored_ref, f, a))

    total = lax.dot_general(
        jnp.full((8, 128), scale, jnp.float32),
        sums_ref[...],
        (((1,), (1,)), ((), ())),
        precision=lax.Precision.HIGHEST,
        preferred_element_type=jnp.float32,
    )
    gram_ref[...] = jnp.broadcast_to(total[:1].reshape(1, 1, 128), gram_ref.shape)


def cost(us):
    return pl.CostEstimate(flops=int(us * 1e9), bytes_accessed=0, transcendentals=0)


def shares(snapshots, freq_ids):
    groups = lax.axis_size("block")
    chips = groups // 2
    block = lax.axis_index("block")
    held = jnp.transpose(snapshots[0], (0, 1, 3, 2, 4))
    owners, _, _, local, _ = held.shape

    def along(value, k):
        route = [(j, (j + 2 * k) % groups) for j in range(groups)]
        return lax.ppermute(value, "block", route)

    table = pl.pallas_call(
        functools.partial(table_kernel, chips, local),
        out_shape=jax.ShapeDtypeStruct((2, chips * ROWS, 12 * local), jnp.bfloat16),
        in_specs=[SMEM, SMEM],
        out_specs=VMEM,
        compiler_params=PARAMS,
        name="table",
    )(block.reshape(1), freq_ids)
    lines, start = [], 0
    for step in PARTS:
        if start:
            held, table = lax.optimization_barrier((held, table))
        mine = held[start : start + step]
        lines.append((mine, lax.ppermute(mine, "block", [(i, i ^ 1) for i in range(groups)])))
        start += step

    total, previous, passed = None, None, []
    for part, (mine, other) in enumerate(lines):
        direct, joined = ((chips - 1, 1), (1, chips - 1))[part]
        if part:
            other, previous = lax.optimization_barrier((other, previous))
        shape = (mine.shape[0] // 2, PAIR, P_SIZE)
        results = pl.pallas_call(
            share_kernel,
            out_shape=[
                jax.ShapeDtypeStruct(shape, jnp.float32 if k in (0, joined) else jnp.bfloat16)
                for k in range(chips)
            ],
            in_specs=[VMEM, HBM, VMEM],
            out_specs=[VMEM] * chips,
            scratch_shapes=[
                pltpu.VMEM(mine.shape, jnp.bfloat16),
                pltpu.SemaphoreType.DMA((FETCHES,)),
            ],
            compiler_params=PARAMS,
            cost_estimate=cost(SHARE_US[part]),
            name="share",
        )(mine, other, table)
        previous = results[0]
        passing = along(results[2], joined)
        sent = along(results[direct], direct)
        if part:
            earlier = [total]
        else:
            earlier = []
        passing, sent = lax.optimization_barrier((passing, sent))
        total = pl.pallas_call(
            join_kernel,
            out_shape=jax.ShapeDtypeStruct(shape, jnp.bfloat16),
            in_specs=[VMEM] * 2 + [ANY] * len(earlier),
            out_specs=VMEM,
            compiler_params=PARAMS,
            cost_estimate=cost(JOIN_US),
            name="join",
        )(results[joined], passing, *earlier)
        passed.append((results[0], sent, along(total, joined)))
    velocity = []
    for part, operands in enumerate(passed):
        velocity = [
            pl.pallas_call(
                sum_kernel,
                out_shape=jax.ShapeDtypeStruct((sum(PARTS[: part + 1]), PAIR, 128), jnp.bfloat16),
                in_specs=[VMEM] * (3 + part),
                out_specs=VMEM,
                compiler_params=PARAMS,
                cost_estimate=cost(SUM_US[part]),
                name="sum",
            )(*operands, *velocity)
        ]
    return velocity[0]


def placing(slot_line):
    me = lax.axis_index("space")
    ids = lax.dynamic_index_in_dim(slot_line, me, 1, keepdims=False)
    place = jnp.arange(ROWS, dtype=jnp.int32)
    in_row = jnp.where(me % 2 == 0, place, jnp.where(place < 32, place + 4, place - 32))
    held = jnp.where(in_row[None, :] < 18, ids[:, 0:1], ids[:, 1:2])
    inner = in_row % 18
    source = (inner % 6 * 3 + inner // 6)[None, :] * LD + held
    real = place < 36
    source = jnp.where((held >= 0) & real[None, :], source, -1).reshape(1, -1)
    target = jnp.arange(18 * LD, dtype=jnp.int32)[:, None]
    return (source == target).astype(jnp.bfloat16)


def per_device(snapshots, slot_line, freq_ids, metrics, weights, stored_spectra):
    groups = lax.axis_size("block")
    holders = lax.axis_size("space")
    velocity = shares(snapshots, freq_ids)
    velocity = lax.all_to_all(velocity, "space", split_axis=0, concat_axis=0, tiled=True)

    nf = NF // groups
    own, low, high = pl.pallas_call(
        place_kernel,
        out_shape=[
            jax.ShapeDtypeStruct((2 * nf, 3, JD, NK, P_SIZE), jnp.bfloat16),
            jax.ShapeDtypeStruct((2 * nf, 3, 2, NK, P_SIZE), jnp.bfloat16),
            jax.ShapeDtypeStruct((2 * nf, 3, 2, NK, P_SIZE), jnp.bfloat16),
        ],
        in_specs=[VMEM, VMEM],
        out_specs=[VMEM, VMEM, VMEM],
        scratch_shapes=[pltpu.VMEM((holders, ROWS, P_SIZE), jnp.bfloat16)],
        compiler_params=PARAMS,
        name="place",
    )(placing(slot_line), velocity)
    forward = [(i, (i + 1) % holders) for i in range(holders)]
    backward = [(target, source) for source, target in forward]
    low = lax.ppermute(low, "space", forward)
    high = lax.ppermute(high, "space", backward)
    base = pl.pallas_call(
        within_kernel,
        out_shape=jax.ShapeDtypeStruct((2 * nf, 3, JD, NK, P_SIZE), jnp.float32),
        in_specs=[VMEM] * 3,
        out_specs=VMEM,
        compiler_params=PARAMS,
        cost_estimate=cost(5),
        name="within",
    )(own, line_matrix(), metrics)
    before = pl.pallas_call(
        stored_kernel,
        out_shape=jax.ShapeDtypeStruct((128, 128), jnp.float32),
        in_specs=[VMEM] * 2,
        out_specs=VMEM,
        compiler_params=PARAMS,
        cost_estimate=cost(1),
        name="stored",
    )(weights, stored_spectra)

    spectra, gram = pl.pallas_call(
        functools.partial(vorticity_kernel, 1.0 / (3.0 * JD * holders * NK * P_SIZE)),
        out_shape=[
            jax.ShapeDtypeStruct((nf, 2, 3, JD, NK, P_SIZE), jnp.bfloat16),
            jax.ShapeDtypeStruct((holders, 1, 128), jnp.float32),
        ],
        in_specs=[VMEM] * 8,
        out_specs=[VMEM, VMEM],
        scratch_shapes=[pltpu.VMEM((128, 128), jnp.float32)],
        compiler_params=PARAMS,
        name="vorticity",
    )(own, low, high, base, metrics, weights, stored_spectra, before)
    gram = lax.all_to_all(gram, "space", split_axis=0, concat_axis=0, tiled=True)
    gram = jnp.sum(gram, axis=(0, 1))[: nf * 18].reshape(nf, 2, 3, 3)
    return (spectra, gram)


def solution(mesh):
    return jax.shard_map(
        per_device,
        mesh=mesh,
        in_specs=(
            P("space", None, None, "block", None, None),
            P(),
            P(),
            P(None, "space", None),
            P("space", None),
            P("block", None, None, None, "space", None, None),
        ),
        out_specs=(P("block", None, None, "space", None, None), P("block", None, None, None)),
        check_vma=False,
    )
```

```python
import functools
import math

import jax
import jax.numpy as jnp
import numpy as np
from jax import lax
from jax.experimental import pallas as pl
from jax.experimental.pallas import tpu as pltpu
from jax.sharding import PartitionSpec as P

P_SIZE = 256
NT = 256
NF = 24
NK = 8
JD = 4
LD = JD * NK
ROWS = 40
PAIR = 72
PARTS = (18, 14)
SHARE_US, JOIN_US, SUM_US = (20, 1), 1, (20, 1)
VMEM = pl.BlockSpec(memory_space=pltpu.VMEM)
SMEM = pl.BlockSpec(memory_space=pltpu.SMEM)
ANY = pl.BlockSpec(memory_space=pl.ANY)
HBM = pl.BlockSpec(memory_space=pltpu.HBM)
FETCHES = 4
PARAMS = pltpu.CompilerParams(vmem_limit_bytes=16 * 1024 * 1024)


def line_matrix():
    d = np.zeros((P_SIZE, P_SIZE), np.float32)
    for p in range(2, P_SIZE - 2):
        d[p - 2, p], d[p - 1, p], d[p + 1, p], d[p + 2, p] = 1, -8, 8, -1
    first, second = (-25, 48, -36, 16, -3), (-3, -10, 18, -6, 1)
    for i in range(5):
        d[i, 0], d[i, 1] = first[i], second[i]
        d[P_SIZE - 1 - i, P_SIZE - 1], d[P_SIZE - 1 - i, P_SIZE - 2] = -first[i], -second[i]
    return jnp.asarray(d, jnp.bfloat16)


def table_kernel(chips, local, block_ref, freq_ref, table_ref):
    block = block_ref[0]
    half = 6 * local
    lane = lax.broadcasted_iota(jnp.int32, (NF, 2 * half), 1)
    far = (lane >= half).astype(jnp.int32)
    time = (block ^ far) * local + ((lane - far * half) & (local - 1))
    row = lax.broadcasted_iota(jnp.int32, (NF, 2 * half), 0)
    freq = jnp.zeros_like(row)
    for f in range(NF):
        freq = jnp.where(row == f, freq_ref[f], freq)
    theta = 2.0 * math.pi / NT * ((time * freq) & (NT - 1)).astype(jnp.float32)
    window = 0.5 - 0.5 * jnp.cos(2.0 * math.pi / NT * time.astype(jnp.float32))
    scale = 1.0 / math.sqrt(0.375 * NT)
    waves = jnp.concatenate(
        [scale * window * jnp.cos(theta), -scale * window * jnp.sin(theta)], axis=0
    ).astype(jnp.bfloat16)

    def line_of(row):
        return sum((row >= 6 * i).astype(jnp.int32) for i in range(1, 6))

    lane = lax.broadcasted_iota(jnp.int32, (ROWS, 2 * half), 1)
    lane_line = line_of((lane - jnp.where(lane >= half, half, 0)) * 6 // local)
    wide = lax.broadcasted_iota(jnp.int32, (ROWS, 2 * half), 0)
    narrow = lax.broadcasted_iota(jnp.int32, (ROWS, 2 * NF), 0)
    wave = lax.broadcasted_iota(jnp.int32, (ROWS, 2 * NF), 1)
    for parity in range(2):
        row = wide - 4 * parity
        kept = (line_of(row) == lane_line) & (row >= 0) & (row < 36)
        row = narrow - 4 * parity
        real = row - 6 * line_of(row)
        for k in range(chips):
            group = ((block >> 1) + k) % chips * 2 + (block & 1)
            pick = wave == group * 3 + (real >> 1) + NF * (real & 1)
            pick = pick.astype(jnp.float32).astype(jnp.bfloat16)
            rows = jnp.dot(pick, waves, preferred_element_type=jnp.float32)
            rows = jnp.where(kept, rows, 0.0).astype(jnp.bfloat16)
            table_ref[parity, k * ROWS : (k + 1) * ROWS] = rows


def share_kernel(mine_ref, other_ref, table_ref, *refs):
    *out_refs, fetched_ref, sems = refs

    def share(d, parity):
        lines = jnp.concatenate(
            [mine_ref[d].reshape(-1, P_SIZE), fetched_ref[d].reshape(-1, P_SIZE)], axis=0
        )
        return jnp.dot(table_ref[parity], lines, preferred_element_type=jnp.float32)

    def step(pair, carry):
        even, odd = share(2 * pair, 0), share(2 * pair + 1, 1)
        for k, ref in enumerate(out_refs):
            first, second = even[k * ROWS : (k + 1) * ROWS], odd[k * ROWS : (k + 1) * ROWS]
            both = jnp.concatenate(
                [first[: ROWS - 8], first[ROWS - 8 :] + second[:8], second[8:]], axis=0
            )
            ref[pair] = both.astype(ref.dtype)
        return carry

    pairs = out_refs[0].shape[0]
    ends = [pairs * (i + 1) // FETCHES for i in range(FETCHES)]
    copies = []
    for i, (start, end) in enumerate(zip([0] + ends, ends)):
        owners = pl.ds(2 * start, 2 * (end - start))
        copies.append(
            pltpu.make_async_copy(other_ref.at[owners], fetched_ref.at[owners], sems.at[i])
        )
        copies[-1].start()
    for copy, start, end in zip(copies, [0] + ends, ends):
        copy.wait()
        lax.fori_loop(start, end, step, 0, unroll=2)


def join_kernel(kept_ref, passing_ref, *refs):
    out_ref = refs[-1]

    def step(pair, carry):
        total = kept_ref[pair] + passing_ref[pair].astype(jnp.float32)
        out_ref[pair] = total.astype(jnp.bfloat16)
        return carry

    lax.fori_loop(0, out_ref.shape[0], step, 0)


def sum_kernel(own_ref, sent_ref, joined_ref, *refs):
    *before_refs, out_ref = refs
    start = 0
    for before_ref in before_refs:
        start = before_ref.shape[0]
        out_ref[:start] = before_ref[...]
    low = lax.broadcasted_iota(jnp.int32, (8, 128), 0) < 4

    def step(pair, carry):
        total = own_ref[pair] + sent_ref[pair].astype(jnp.float32)
        total = total + joined_ref[pair].astype(jnp.float32)
        left, right = total[:, :128], total[:, 128:]
        middle = slice(32, 40)
        even = jnp.where(low, left[middle], pltpu.roll(right[middle], 4, 0))
        odd = jnp.where(low, pltpu.roll(left[middle], 4, 0), right[middle])
        for i, mixed, rows in ((0, even, slice(0, 32)), (1, odd, slice(40, 72))):
            block = jnp.concatenate([left[rows], mixed, right[rows]], axis=0)
            out_ref[start + 2 * pair + i] = block.astype(jnp.bfloat16)
        return carry

    lax.fori_loop(0, own_ref.shape[0], step, 0)


def place_kernel(place_ref, packed_ref, own_ref, low_ref, high_ref, held_ref):
    def unpack(h, carry):
        mixed = packed_ref[h, 32:40].astype(jnp.float32)
        turned = pltpu.roll(mixed, 4, 0).astype(jnp.bfloat16)
        held_ref[h, :, :128] = packed_ref[h, :40]
        held_ref[h, :, 128:] = jnp.concatenate([packed_ref[h, 40:], turned], axis=0)
        return carry

    lax.fori_loop(0, packed_ref.shape[0], unpack, 0, unroll=2)
    held = held_ref[...].reshape(-1, P_SIZE)
    rows = jnp.dot(place_ref[...], held, preferred_element_type=jnp.float32)
    rows = rows.astype(jnp.bfloat16).reshape(own_ref.shape)
    own_ref[...] = rows
    low_ref[...] = rows[:, :, JD - 2 :]
    high_ref[...] = rows[:, :, :2]


def add_products(sums_ref, f, a, b, left, right):
    def put(part, value):
        total = jnp.sum(value, axis=(0, 1, 2)).reshape(1, P_SIZE)
        total = total[:, :128] + total[:, 128:]
        row = ((f * 2 + part) * 3 + a) * 3 + b
        sums_ref[pl.ds(row, 1), :] = total
        if a != b:
            row = ((f * 2 + part) * 3 + b) * 3 + a
            sums_ref[pl.ds(row, 1), :] = total if part == 0 else -total

    put(0, left[0] * right[0] + left[1] * right[1])
    if a != b:
        put(1, left[0] * right[1] - left[1] * right[0])


def column(ref, f, a):
    return tuple(ref[f, a, r].astype(jnp.float32) for r in range(2))


def stored_kernel(weight_ref, stored_ref, sums_ref):
    sums_ref[...] = jnp.zeros_like(sums_ref)
    weight = weight_ref[...].reshape(1, JD, 1, P_SIZE)
    for f in range(stored_ref.shape[0]):
        columns = [column(stored_ref, f, a) for a in range(2)]
        for a in range(2):
            left = tuple(weight * v for v in columns[a])
            for b in range(a, 2):
                add_products(sums_ref, f, a + 1, b + 1, left, columns[b])


def within_kernel(own_ref, line_ref, metric_ref, base_ref):
    xi_x, xi_y = (metric_ref[i].reshape(JD, 1, P_SIZE) for i in range(2))
    twelfth = 1.0 / 12.0
    for q in range(own_ref.shape[0]):
        along, span = [], []
        for c in range(3):
            line = own_ref[q, c].reshape(LD, P_SIZE)
            value = jnp.dot(line, line_ref[...], preferred_element_type=jnp.float32)
            along.append((value * twelfth).reshape(JD, NK, P_SIZE))
        for c in range(2):
            center = own_ref[q, c].astype(jnp.float32)
            value = (
                pltpu.roll(center, 2, 1)
                - 8.0 * pltpu.roll(center, 1, 1)
                + 8.0 * pltpu.roll(center, NK - 1, 1)
                - pltpu.roll(center, NK - 2, 1)
            )
            span.append(value * twelfth)
        base_ref[q, 0] = xi_y * along[2] - span[1]
        base_ref[q, 1] = span[0] - xi_x * along[2]
        base_ref[q, 2] = xi_x * along[1] - xi_y * along[0]


def vorticity_kernel(
    scale,
    own_ref,
    low_ref,
    high_ref,
    base_ref,
    metric_ref,
    weight_ref,
    stored_ref,
    before_ref,
    spectra_ref,
    gram_ref,
    sums_ref,
):
    sums_ref[...] = before_ref[...]
    eta_x, eta_y = (metric_ref[i].reshape(JD, 1, P_SIZE) * (1.0 / 12.0) for i in (2, 3))
    weight = weight_ref[...].reshape(1, JD, 1, P_SIZE)

    def step(f, carry):
        new = []
        for r in range(2):
            q = 2 * f + r
            pitch = []
            for c in range(3):
                padded = jnp.concatenate(
                    [ref[q, c].astype(jnp.float32) for ref in (low_ref, own_ref, high_ref)],
                    axis=0,
                )
                pitch.append(padded[:-4] - 8.0 * padded[1:-3] + 8.0 * padded[3:-1] - padded[4:])
            vort = [
                base_ref[q, 0] + eta_y * pitch[2],
                base_ref[q, 1] - eta_x * pitch[2],
                base_ref[q, 2] + eta_x * pitch[1] - eta_y * pitch[0],
            ]
            vort = [v.astype(jnp.bfloat16) for v in vort]
            for c in range(3):
                spectra_ref[f, r, c] = vort[c]
            new.append(jnp.stack([v.astype(jnp.float32) for v in vort], axis=0))
        left = tuple(weight * v for v in new)
        add_products(sums_ref, f, 0, 0, left, new)
        for a in range(2):
            add_products(sums_ref, f, 0, a + 1, left, column(stored_ref, f, a))
        return carry

    lax.fori_loop(0, stored_ref.shape[0], step, 0)

    total = lax.dot_general(
        jnp.full((8, 128), scale, jnp.float32),
        sums_ref[...],
        (((1,), (1,)), ((), ())),
        precision=lax.Precision.HIGHEST,
        preferred_element_type=jnp.float32,
    )
    gram_ref[...] = jnp.broadcast_to(total[:1].reshape(1, 1, 128), gram_ref.shape)


def cost(us):
    return pl.CostEstimate(flops=int(us * 1e9), bytes_accessed=0, transcendentals=0)


def shares(snapshots, freq_ids):
    groups = lax.axis_size("block")
    chips = groups // 2
    block = lax.axis_index("block")
    held = jnp.transpose(snapshots[0], (0, 1, 3, 2, 4))
    owners, _, _, local, _ = held.shape

    def along(value, k):
        route = [(j, (j + 2 * k) % groups) for j in range(groups)]
        return lax.ppermute(value, "block", route)

    table = pl.pallas_call(
        functools.partial(table_kernel, chips, local),
        out_shape=jax.ShapeDtypeStruct((2, chips * ROWS, 12 * local), jnp.bfloat16),
        in_specs=[SMEM, SMEM],
        out_specs=VMEM,
        compiler_params=PARAMS,
        name="table",
    )(block.reshape(1), freq_ids)
    lines, start = [], 0
    for step in PARTS:
        if start:
            held, table = lax.optimization_barrier((held, table))
        mine = held[start : start + step]
        lines.append((mine, lax.ppermute(mine, "block", [(i, i ^ 1) for i in range(groups)])))
        start += step

    total, previous, passed = None, None, []
    for part, (mine, other) in enumerate(lines):
        direct, joined = ((chips - 1, 1), (1, chips - 1))[part]
        if part:
            other, previous = lax.optimization_barrier((other, previous))
        shape = (mine.shape[0] // 2, PAIR, P_SIZE)
        results = pl.pallas_call(
            share_kernel,
            out_shape=[
                jax.ShapeDtypeStruct(shape, jnp.float32 if k in (0, joined) else jnp.bfloat16)
                for k in range(chips)
            ],
            in_specs=[VMEM, HBM, VMEM],
            out_specs=[VMEM] * chips,
            scratch_shapes=[
                pltpu.VMEM(mine.shape, jnp.bfloat16),
                pltpu.SemaphoreType.DMA((FETCHES,)),
            ],
            compiler_params=PARAMS,
            cost_estimate=cost(SHARE_US[part]),
            name="share",
        )(mine, other, table)
        previous = results[0]
        passing = along(results[2], joined)
        sent = along(results[direct], direct)
        if part:
            earlier = [total]
        else:
            earlier = []
        passing, sent = lax.optimization_barrier((passing, sent))
        total = pl.pallas_call(
            join_kernel,
            out_shape=jax.ShapeDtypeStruct(shape, jnp.bfloat16),
            in_specs=[VMEM] * 2 + [ANY] * len(earlier),
            out_specs=VMEM,
            compiler_params=PARAMS,
            cost_estimate=cost(JOIN_US),
            name="join",
        )(results[joined], passing, *earlier)
        passed.append((results[0], sent, along(total, joined)))
    velocity = []
    for part, operands in enumerate(passed):
        velocity = [
            pl.pallas_call(
                sum_kernel,
                out_shape=jax.ShapeDtypeStruct((sum(PARTS[: part + 1]), PAIR, 128), jnp.bfloat16),
                in_specs=[VMEM] * (3 + part),
                out_specs=VMEM,
                compiler_params=PARAMS,
                cost_estimate=cost(SUM_US[part]),
                name="sum",
            )(*operands, *velocity)
        ]
    return velocity[0]


def placing(slot_line):
    me = lax.axis_index("space")
    ids = lax.dynamic_index_in_dim(slot_line, me, 1, keepdims=False)
    place = jnp.arange(ROWS, dtype=jnp.int32)
    in_row = jnp.where(me % 2 == 0, place, jnp.where(place < 32, place + 4, place - 32))
    held = jnp.where(in_row[None, :] < 18, ids[:, 0:1], ids[:, 1:2])
    inner = in_row % 18
    source = (inner % 6 * 3 + inner // 6)[None, :] * LD + held
    real = place < 36
    source = jnp.where((held >= 0) & real[None, :], source, -1).reshape(1, -1)
    target = jnp.arange(18 * LD, dtype=jnp.int32)[:, None]
    return (source == target).astype(jnp.bfloat16)


def per_device(snapshots, slot_line, freq_ids, metrics, weights, stored_spectra):
    groups = lax.axis_size("block")
    holders = lax.axis_size("space")
    velocity = shares(snapshots, freq_ids)
    velocity = lax.all_to_all(velocity, "space", split_axis=0, concat_axis=0, tiled=True)

    nf = NF // groups
    own, low, high = pl.pallas_call(
        place_kernel,
        out_shape=[
            jax.ShapeDtypeStruct((2 * nf, 3, JD, NK, P_SIZE), jnp.bfloat16),
            jax.ShapeDtypeStruct((2 * nf, 3, 2, NK, P_SIZE), jnp.bfloat16),
            jax.ShapeDtypeStruct((2 * nf, 3, 2, NK, P_SIZE), jnp.bfloat16),
        ],
        in_specs=[VMEM, VMEM],
        out_specs=[VMEM, VMEM, VMEM],
        scratch_shapes=[pltpu.VMEM((holders, ROWS, P_SIZE), jnp.bfloat16)],
        compiler_params=PARAMS,
        name="place",
    )(placing(slot_line), velocity)
    forward = [(i, (i + 1) % holders) for i in range(holders)]
    backward = [(target, source) for source, target in forward]
    low = lax.ppermute(low, "space", forward)
    high = lax.ppermute(high, "space", backward)
    base = pl.pallas_call(
        within_kernel,
        out_shape=jax.ShapeDtypeStruct((2 * nf, 3, JD, NK, P_SIZE), jnp.float32),
        in_specs=[VMEM] * 3,
        out_specs=VMEM,
        compiler_params=PARAMS,
        cost_estimate=cost(5),
        name="within",
    )(own, line_matrix(), metrics)
    before = pl.pallas_call(
        stored_kernel,
        out_shape=jax.ShapeDtypeStruct((128, 128), jnp.float32),
        in_specs=[VMEM] * 2,
        out_specs=VMEM,
        compiler_params=PARAMS,
        cost_estimate=cost(1),
        name="stored",
    )(weights, stored_spectra)

    spectra, gram = pl.pallas_call(
        functools.partial(vorticity_kernel, 1.0 / (3.0 * JD * holders * NK * P_SIZE)),
        out_shape=[
            jax.ShapeDtypeStruct((nf, 2, 3, JD, NK, P_SIZE), jnp.bfloat16),
            jax.ShapeDtypeStruct((holders, 1, 128), jnp.float32),
        ],
        in_specs=[VMEM] * 8,
        out_specs=[VMEM, VMEM],
        scratch_shapes=[pltpu.VMEM((128, 128), jnp.float32)],
        compiler_params=PARAMS,
        name="vorticity",
    )(own, low, high, base, metrics, weights, stored_spectra, before)
    gram = lax.all_to_all(gram, "space", split_axis=0, concat_axis=0, tiled=True)
    gram = jnp.sum(gram, axis=(0, 1))[: nf * 18].reshape(nf, 2, 3, 3)
    return (spectra, gram)


def solution(mesh):
    return jax.shard_map(
        per_device,
        mesh=mesh,
        in_specs=(
            P("space", None, None, "block", None, None),
            P(),
            P(),
            P(None, "space", None),
            P("space", None),
            P("block", None, None, None, "space", None, None),
        ),
        out_specs=(P("block", None, None, "space", None, None), P("block", None, None, None)),
        check_vma=False,
    )
```
